256 devices in a mesh: dp: 4 (over y), wide: 16 (over x_hi, z), narrow: 4 (over x_lo, core).
Axes of the slice: x: 4 (x_hi: 2, x_lo: 2; x = x_hi * 2 + x_lo), y: 4, z: 8, core: 2. Of those that a mesh axis runs over, the one named last changes fastest.
Arguments:
- tokens: bfloat16 [512, 256, 1280], P(('dp', 'wide', 'narrow')), may hold values from -20 to 20
- router: bfloat16 [1280, 128], replicated, may hold values from -1 to 1
- expert_in: bfloat16 [64, 1280, 2560], P(('wide', 'narrow'), None, 'dp'), may hold values from -0.15625 to 0.15625
- expert_out: bfloat16 [64, 2560, 1280], P(('wide', 'narrow'), 'dp'), may hold values from -0.125 to 0.125
- cotangent: bfloat16 [512, 256, 1280], P(('dp', 'wide', 'narrow')), may hold values from -6 to 6
Outputs:
- mixed: bfloat16 [512, 256, 1280], P(('dp', 'wide', 'narrow'))
- token_grad: bfloat16 [512, 256, 1280], P(('dp', 'wide', 'narrow'))
- router_grad: float32 [1280, 128], replicated
- grad_in: bfloat16 [64, 1280, 2560], P(('wide', 'narrow'), None, 'dp')
- grad_out: bfloat16 [64, 2560, 1280], P(('wide', 'narrow'), 'dp')
The draws below stay inside these ranges and needn't reach their ends.
All inputs are finite; a program needn't handle non-finite values.
Results may differ from the reference program's by a relative error of at most 0.018.
Values may be sent and summed in bfloat16 or wider, within the bound.
A program may use at most 128 MiB of HBM per device.

```python
import math
import jax
import jax.numpy as jnp
from jax import lax

D = 1280
HID = 2560
TOK = 256
SPE = 2
EXPERTS = 64
SLOTS = 128
IMAGES = 512
N_DP = 4


def router_table(key):
    key = jax.random.fold_in(key, 11)
    signs = jax.random.randint(key, (D, SLOTS), 0, 2).astype(jnp.float32)
    return (2.0 * signs - 1.0) / math.sqrt(D)


def draw_router(key, part):
    return router_table(key).astype(jnp.bfloat16)


def draw_tokens(key, part):
    key = jax.random.fold_in(key, 3)
    keys = jax.random.split(key, 2)
    scales = jnp.exp(jax.random.uniform(keys[0], (IMAGES, TOK, 1), jnp.float32, math.log(0.4), math.log(4.0)))
    values = jax.random.truncated_normal(keys[1], -4.0, 4.0, (IMAGES, TOK, D), jnp.float32) * scales
    return values.astype(jnp.bfloat16)


def block_levels(key, dims, cuts, smallest, top_value):
    gain = 1.0
    for axis_at, shards_of in cuts:
        draws = jax.random.uniform(jax.random.fold_in(jax.random.fold_in(key, 6), axis_at), (shards_of,), jnp.float32, smallest / len(cuts), top_value / len(cuts))
        gain = gain * jnp.repeat(jnp.exp(draws), dims[axis_at] // shards_of).reshape((-1,) + (1,) * (len(dims) - 1 - axis_at))
    return gain


def centred(rng, shape, width, reach, shards=(), held_as=jnp.bfloat16):
    values = jax.random.normal(rng, shape, jnp.float32) * width
    if len(shards) > 0:
        values = block_levels(rng, shape, shards, -0.22, 0.18) * values
    return jnp.clip(values, min=-reach, max=reach).astype(held_as)


def setup_inputs(seed: int = 0) -> dict:
    key_of = jax.random.split(jax.random.key(seed), 6)
    tokens = draw_tokens(jax.random.fold_in(key_of[5], 71), 0)
    router = draw_router(jax.random.fold_in(key_of[5], 71), 0)
    expert_in = centred(key_of[2], (EXPERTS, D, HID), D ** -0.5, 0.15625, ((0, 64), (2, 4)))
    expert_out = centred(key_of[3], (EXPERTS, HID, D), HID ** -0.5, 0.125, ((0, 64), (1, 4)))
    cotangent = centred(key_of[4], (IMAGES, TOK, D), 1.0, 6.0, ((0, 256),))
    return {"tokens": tokens, "router": router, "expert_in": expert_in, "expert_out": expert_out, "cotangent": cotangent}


def gelu_exact(values):
    return jax.nn.gelu(values, approximate=False)

def image_front(tokens, cotangent, router):
    logits = jnp.dot(tokens, router, preferred_element_type=jnp.float32)
    dispatch = jax.nn.softmax(logits, axis=0)
    combine = jax.nn.softmax(logits, axis=1)
    dispatch_low = dispatch.astype(jnp.bfloat16)
    combine_low = combine.astype(jnp.bfloat16)
    slot_in = jnp.dot(dispatch_low.T, tokens, preferred_element_type=jnp.float32).astype(jnp.bfloat16)
    slot_cot = jnp.dot(combine_low.T, cotangent, preferred_element_type=jnp.float32).astype(jnp.bfloat16)
    return (slot_in, slot_cot)

def image_back(tokens, cotangent, router, slot_out, slot_grad):
    logits = jnp.dot(tokens, router, preferred_element_type=jnp.float32)
    dispatch = jax.nn.softmax(logits, axis=0)
    combine = jax.nn.softmax(logits, axis=1)
    dispatch_low = dispatch.astype(jnp.bfloat16)
    combine_low = combine.astype(jnp.bfloat16)
    mixed = jnp.dot(combine_low, slot_out, preferred_element_type=jnp.float32).astype(jnp.bfloat16)
    left = jnp.dot(cotangent, slot_out.T, preferred_element_type=jnp.float32)
    right = jnp.dot(tokens, slot_grad.T, preferred_element_type=jnp.float32)
    part_combine = combine * (left - lax.optimization_barrier(jnp.sum(combine * left, axis=1, keepdims=True)))
    part_dispatch = dispatch * (right - lax.optimization_barrier(jnp.sum(dispatch * right, axis=0, keepdims=True)))
    logit_grad = (part_combine + part_dispatch).astype(jnp.bfloat16)
    token_grad = jnp.dot(dispatch_low, slot_grad, preferred_element_type=jnp.float32)
    token_grad = token_grad + jnp.dot(logit_grad, router.T, preferred_element_type=jnp.float32)
    router_term = jnp.dot(tokens.T, logit_grad, preferred_element_type=jnp.float32)
    return (mixed, token_grad.astype(jnp.bfloat16), router_term)

def expert_pass(items):
    rows, cots, first, second = items
    flat_rows = rows.reshape(-1, D)
    flat_cots = cots.reshape(-1, D)
    pre = jnp.dot(flat_rows, first, preferred_element_type=jnp.float32)
    active, pullback = jax.vjp(gelu_exact, pre)
    act_low = active.astype(jnp.bfloat16)
    slot_out = jnp.dot(act_low, second, preferred_element_type=jnp.float32).astype(jnp.bfloat16)
    back = jnp.dot(flat_cots, second.T, preferred_element_type=jnp.float32)
    hidden_grad = pullback(back)[0].astype(jnp.bfloat16)
    slot_grad = jnp.dot(hidden_grad, first.T, preferred_element_type=jnp.float32).astype(jnp.bfloat16)
    group_hidden = hidden_grad.reshape(N_DP, -1, HID).astype(jnp.float32)
    group_act = act_low.reshape(N_DP, -1, HID).astype(jnp.float32)
    terms_first = jnp.einsum('grd,grh->gdh', rows.astype(jnp.float32), group_hidden).astype(jnp.bfloat16)
    terms_second = jnp.einsum('grh,grd->ghd', group_act, cots.astype(jnp.float32)).astype(jnp.bfloat16)
    terms_first, terms_second = lax.optimization_barrier((terms_first, terms_second))
    grad_first = lax.optimization_barrier(jnp.sum(terms_first.astype(jnp.float32), axis=0)).astype(jnp.bfloat16)
    grad_second = lax.optimization_barrier(jnp.sum(terms_second.astype(jnp.float32), axis=0)).astype(jnp.bfloat16)
    return (slot_out.reshape(N_DP, -1, D), slot_grad.reshape(N_DP, -1, D), grad_first, grad_second)

def to_experts(slots):
    group_images = IMAGES // N_DP
    shaped = slots.reshape(N_DP, group_images, EXPERTS, SPE, D)
    return shaped.transpose(2, 0, 1, 3, 4).reshape(EXPERTS, N_DP, group_images * SPE, D)

def from_experts(values):
    group_images = IMAGES // N_DP
    shaped = values.reshape(EXPERTS, N_DP, group_images, SPE, D)
    return shaped.transpose(1, 2, 0, 3, 4).reshape(IMAGES, SLOTS, D)

def reference(tokens, router, expert_in, expert_out, cotangent):
    slot_in, slot_cot = jax.vmap(image_front, in_axes=(0, 0, None))(tokens, cotangent, router)
    outs = lax.map(expert_pass, (to_experts(slot_in), to_experts(slot_cot), expert_in, expert_out))
    slot_out = from_experts(outs[0])
    slot_grad = from_experts(outs[1])
    mixed, token_grad, router_terms = jax.vmap(image_back, in_axes=(0, 0, None, 0, 0))(tokens, cotangent, router, slot_out, slot_grad)
    router_grad = lax.optimization_barrier(jnp.sum(router_terms, axis=0))
    return (mixed, token_grad, router_grad, outs[2], outs[3])
```

```python
import jax
import jax.numpy as jnp
from jax import lax
from jax.sharding import PartitionSpec as P

PLANE = ("wide", "narrow")


def gelu_exact(values):
    return jax.nn.gelu(values, approximate=False)


def dot(a, b):
    return jnp.dot(a, b, preferred_element_type=jnp.float32)


def exchange(x):
    return lax.all_to_all(x, PLANE, split_axis=0, concat_axis=0, tiled=True)


def local(tokens, router, expert_in, expert_out, cotangent):
    images, length, width = tokens.shape
    slot_count = router.shape[1]
    n_plane = lax.axis_size("wide") * lax.axis_size("narrow")
    n_dp = lax.axis_size("dp")
    per_expert = slot_count // n_plane
    logits = jnp.einsum("itd,ds->its", tokens, router, preferred_element_type=jnp.float32)
    dispatch = jax.nn.softmax(logits, axis=1)
    combine = jax.nn.softmax(logits, axis=2)
    dispatch_low = dispatch.astype(jnp.bfloat16)
    combine_low = combine.astype(jnp.bfloat16)
    slot_in = jnp.einsum(
        "its,itd->sid", dispatch_low, tokens, preferred_element_type=jnp.float32
    ).astype(jnp.bfloat16)
    slot_cot = jnp.einsum(
        "its,itd->sid", combine_low, cotangent, preferred_element_type=jnp.float32
    ).astype(jnp.bfloat16)
    shape = (n_plane, per_expert * images, width)
    rows = lax.all_gather(exchange(slot_in.reshape(shape)).reshape(-1, width), "dp", axis=0, tiled=True)
    cots = lax.all_gather(exchange(slot_cot.reshape(shape)).reshape(-1, width), "dp", axis=0, tiled=True)

    first, second = expert_in[0], expert_out[0]
    pre = dot(rows, first)
    active, pullback = jax.vjp(gelu_exact, pre)
    act_low = active.astype(jnp.bfloat16)
    out_part = dot(act_low, second).astype(jnp.bfloat16)
    slot_out = lax.psum_scatter(out_part, "dp", scatter_dimension=0, tiled=True)
    back = lax.dot_general(cots, second, (((1,), (1,)), ((), ())), preferred_element_type=jnp.float32)
    hidden_grad = pullback(back)[0].astype(jnp.bfloat16)
    grad_part = lax.dot_general(
        hidden_grad, first, (((1,), (1,)), ((), ())), preferred_element_type=jnp.float32
    ).astype(jnp.bfloat16)
    slot_grad = lax.psum_scatter(grad_part, "dp", scatter_dimension=0, tiled=True)
    grad_in = lax.dot_general(
        rows, hidden_grad, (((0,), (0,)), ((), ())), preferred_element_type=jnp.float32
    ).astype(jnp.bfloat16)
    grad_out = lax.dot_general(
        act_low, cots, (((0,), (0,)), ((), ())), preferred_element_type=jnp.float32
    ).astype(jnp.bfloat16)

    outs_back = exchange(slot_out.reshape(shape)).reshape(slot_count, images, width)
    grads_back = exchange(slot_grad.reshape(shape)).reshape(slot_count, images, width)
    mixed = jnp.einsum(
        "its,sid->itd", combine_low, outs_back, preferred_element_type=jnp.float32
    ).astype(jnp.bfloat16)
    left = jnp.einsum("itd,sid->its", cotangent, outs_back, preferred_element_type=jnp.float32)
    right = jnp.einsum("itd,sid->its", tokens, grads_back, preferred_element_type=jnp.float32)
    part_combine = combine * (left - jnp.sum(combine * left, axis=2, keepdims=True))
    part_dispatch = dispatch * (right - jnp.sum(dispatch * right, axis=1, keepdims=True))
    logit_grad = (part_combine + part_dispatch).astype(jnp.bfloat16)
    token_grad = jnp.einsum(
        "its,sid->itd", dispatch_low, grads_back, preferred_element_type=jnp.float32
    )
    token_grad = token_grad + jnp.einsum(
        "its,ds->itd", logit_grad, router, preferred_element_type=jnp.float32
    )
    router_local = jnp.einsum("itd,its->ds", tokens, logit_grad, preferred_element_type=jnp.float32)
    share = exchange(router_local.reshape(n_plane, -1, slot_count))
    share = lax.psum(jnp.sum(share, axis=0), "dp")
    router_grad = lax.all_gather(share, PLANE, axis=0, tiled=True)
    return (mixed, token_grad.astype(jnp.bfloat16), router_grad, grad_in[None], grad_out[None])


def solution(mesh):
    in_specs = (
        P(("dp", "wide", "narrow"), None, None),
        P(),
        P(("wide", "narrow"), None, "dp"),
        P(("wide", "narrow"), "dp", None),
        P(("dp", "wide", "narrow"), None, None),
    )
    out_specs = (
        P(("dp", "wide", "narrow"), None, None),
        P(("dp", "wide", "narrow"), None, None),
        P(),
        P(("wide", "narrow"), None, "dp"),
        P(("wide", "narrow"), "dp", None),
    )
    return jax.shard_map(local, mesh=mesh, in_specs=in_specs, out_specs=out_specs, check_vma=False)
```

```python
import functools

import jax
import jax.numpy as jnp
from jax import lax
from jax.experimental import pallas as pl
from jax.experimental.pallas import tpu as pltpu
from jax.sharding import PartitionSpec as P

MESH = pl.DeviceIdType.MESH
BF = jnp.bfloat16
F32 = jnp.float32
PH = 4
HALF = 640


def dot(a, b):
    return jnp.dot(a, b, preferred_element_type=F32)


def dot_nt(a, b):
    return lax.dot_general(a, b, (((1,), (1,)), ((), ())), preferred_element_type=F32)


def dot_tn(a, b):
    return lax.dot_general(a, b, (((0,), (0,)), ((), ())), preferred_element_type=F32)


def normal_cdf_pdf(x):
    z = jnp.abs(x) * 0.7071067811865476
    t = 1.0 / (1.0 + 0.5 * z)
    poly = 0.17087277
    for c in (
        -0.82215223,
        1.48851587,
        -1.13520398,
        0.27886807,
        -0.18628806,
        0.09678418,
        0.37409196,
        1.00002368,
        -1.26551223,
    ):
        poly = poly * t + c
    square = z * z
    tail = 0.5 * t * jnp.exp(poly - square)
    cdf = jnp.where(x < 0, tail, 1.0 - tail)
    pdf = 0.3989422804014327 * jnp.exp(-square)
    return cdf, pdf


def kernel(
    tok_h, rout_h, win_h, wout_h, cot_h,
    mixed_h, tg_h, rg_h, gi_h, go_h,
    tok, rout, win, wout, cot,
    perm, perm_t, disp, comb, stage, send, recv, gath, part, ring_a, ring_b, ring_c,
    pre, back_f, act, hid, ret, back, low, mixed, tgrad, ginv, goutv,
    rloc, ar0, half, ar1, ar2, one, fin,
    load_sem, out_sem, own_sem, a2a_send, a2a_recv, ag_send, ag_recv, rs_send, rs_recv,
    ret_send, ret_recv, ar_send, ar_recv,
):
    y = lax.axis_index("dp")
    wide = lax.axis_index("wide")
    narrow = lax.axis_index("narrow")
    me = wide * 4 + narrow
    z = lax.rem(wide, 8)
    x = (wide // 8) * 2 + narrow // 2
    core = lax.rem(narrow, 2)
    spot = y * 4 + x

    def plane(e):
        return {"wide": e // 4, "narrow": lax.rem(e, 4)}

    def chip(q):
        cx = lax.rem(q, 4)
        return {"dp": q // 4, "wide": (cx // 2) * 8 + z, "narrow": lax.rem(cx, 2) * 2 + core}

    up = {"dp": lax.rem(y + 1, 4)}
    down = {"dp": lax.rem(y + 3, 4)}

    loads = [
        pltpu.make_async_copy(a, b, load_sem.at[i])
        for i, (a, b) in enumerate(
            ((tok_h, tok), (rout_h, rout), (cot_h, cot), (win_h, win), (wout_h, wout))
        )
    ]
    for c in loads:
        c.start()

    barrier = pltpu.get_barrier_semaphore()

    def greet(k, _):
        pl.semaphore_signal(
            barrier, inc=1, device_id=plane(lax.rem(me + k, 64)), device_id_type=MESH
        )
        return _

    lax.fori_loop(1, 64, greet, 0)

    def greet_far(k, _):
        q = lax.rem(y + 1 + k // 4, 4) * 4 + lax.rem(k, 4)
        pl.semaphore_signal(barrier, inc=1, device_id=chip(q), device_id_type=MESH)
        return _

    lax.fori_loop(0, 12, greet_far, 0)

    def source(r):
        e16 = r // 16
        h = (r // 8) % 2
        c = (r // 4) % 2
        s = (r // 2) % 2
        return (h * 4 + c * 2 + r % 2) * 32 + e16 * 2 + s

    i0 = lax.broadcasted_iota(jnp.int32, (256, 256), 0)
    i1 = lax.broadcasted_iota(jnp.int32, (256, 256), 1)
    perm[...] = jnp.where(source(i0) == i1, 1.0, 0.0).astype(BF)
    perm_t[...] = jnp.where(source(i1) == i0, 1.0, 0.0).astype(BF)

    loads[0].wait()
    loads[1].wait()
    for i in range(2):
        rows = pl.ds(i * 256, 256)
        logits = dot(tok[rows, :], rout[...])
        d = jnp.exp(logits - jnp.max(logits, axis=0, keepdims=True))
        d = d / jnp.sum(d, axis=0, keepdims=True)
        c = jnp.exp(logits - jnp.max(logits, axis=1, keepdims=True))
        c = c / jnp.sum(c, axis=1, keepdims=True)
        disp[rows, :] = d
        comb[rows, :] = c
        if i == 0:
            loads[2].wait()
        for kind, (weight, values) in enumerate(((d, tok), (c, cot))):
            weight_t = weight.astype(BF).T
            for h in range(2):
                slots = dot(weight_t, values[rows, pl.ds(h * HALF, HALF)]).astype(BF)
                for g in range(4):
                    stage[g, pl.ds((h * 4 + kind * 2 + i) * 32, 32), :] = slots[
                        g * 32 : g * 32 + 32, :
                    ]
    for g in range(4):
        send[pl.ds(g * 256, 256), :] = dot(perm[...], stage[g]).astype(BF)

    pl.semaphore_wait(barrier, 75)

    own = pltpu.make_async_copy(
        send.at[pl.ds(pl.multiple_of(me * 16, 16), 16)], recv.at[pl.ds(0, 16)], own_sem.at[0]
    )
    own.start()
    for p in range(PH):

        def post(k, _, p=p):
            e = lax.rem(me + k, 64)
            pltpu.make_async_remote_copy(
                src_ref=send.at[pl.ds(pl.multiple_of(e * 16, 16), 16)],
                dst_ref=recv.at[pl.ds(pl.multiple_of(k * 16, 16), 16)],
                send_sem=a2a_send.at[0],
                recv_sem=a2a_recv.at[p],
                device_id=plane(e),
                device_id_type=MESH,
            ).start()
            return _

        lax.fori_loop(max(16 * p, 1), 16 * p + 16, post, 0)

    def wait_bytes(ref, sem):
        pltpu.make_async_copy(ref, ref, sem).wait()

    def remote(src, dst, s, r, to):
        return pltpu.make_async_remote_copy(
            src_ref=src, dst_ref=dst, send_sem=s, recv_sem=r, device_id=to, device_id_type=MESH
        )

    lo, hi = pl.ds(0, 2), pl.ds(2, 2)
    ag = {}
    rs = {}

    def stage_a(p):
        if p == 0:
            own.wait()
            wait_bytes(recv.at[pl.ds(16, 240)], a2a_recv.at[0])
        else:
            wait_bytes(recv.at[pl.ds(256 * p, 256)], a2a_recv.at[p])
        rows = dot(perm_t[...], recv[pl.ds(256 * p, 256), :]).astype(BF)
        gath[p, :, 0] = rows.reshape(4, 64, HALF)
        ag[p, 0] = remote(gath.at[p, :, 0], gath.at[p, :, 1], ag_send.at[p, 0], ag_recv.at[p, 0], up)
        ag[p, 1] = remote(gath.at[p, :, 0], gath.at[p, :, 3], ag_send.at[p, 1], ag_recv.at[p, 1], down)
        ag[p, 0].start()
        ag[p, 1].start()

    def stage_b(p):
        ag[p, 0].wait_recv()
        ag[p, 2] = remote(gath.at[p, lo, 1], gath.at[p, lo, 2], ag_send.at[p, 2], ag_recv.at[p, 2], up)
        ag[p, 2].start()
        ag[p, 1].wait_recv()
        ag[p, 3] = remote(gath.at[p, hi, 3], gath.at[p, hi, 2], ag_send.at[p, 3], ag_recv.at[p, 3], down)
        ag[p, 3].start()

    def stage_c(p):
        ag[p, 2].wait_recv()
        ag[p, 3].wait_recv()
        if p == 0:
            loads[3].wait()
            loads[4].wait()
        mine = pl.ds(256 * p, 256)

        def rows(q):
            return gath[p, q].reshape(256, HALF)

        pre[...] = dot(rows(0), win[pl.ds(0, HALF), :]) + dot(rows(2), win[pl.ds(HALF, HALF), :])
        back_f[...] = dot_nt(rows(1), wout[:, pl.ds(0, HALF)]) + dot_nt(
            rows(3), wout[:, pl.ds(HALF, HALF)]
        )

        def nonlinear(j, _):
            r = pl.ds(pl.multiple_of(j * 16, 16), 16)
            v = pre[r, :]
            cdf, pdf = normal_cdf_pdf(v)
            to = pl.ds(pl.multiple_of(256 * p + j * 16, 16), 16)
            act[to, :] = (v * cdf).astype(BF)
            hid[to, :] = (back_f[r, :] * (cdf + v * pdf)).astype(BF)
            return _

        lax.fori_loop(0, 16, nonlinear, 0)
        for h in range(2):
            cols = pl.ds(h * HALF, HALF)
            part[p, 2 * h] = dot(act[mine, :], wout[:, cols]).astype(BF).reshape(4, 64, HALF)
            part[p, 2 * h + 1] = dot_nt(hid[mine, :], win[cols, :]).astype(BF).reshape(4, 64, HALF)
        rs[p, 0] = remote(part.at[p, lo, 2], ring_a.at[p, 0], rs_send.at[p, 0], rs_recv.at[p, 0], up)
        rs[p, 1] = remote(part.at[p, hi, 2], ring_a.at[p, 1], rs_send.at[p, 1], rs_recv.at[p, 1], down)
        rs[p, 2] = remote(part.at[p, hi, 3], ring_b.at[p, hi], rs_send.at[p, 2], rs_recv.at[p, 2], up)
        rs[p, 3] = remote(part.at[p, lo, 1], ring_c.at[p, lo], rs_send.at[p, 3], rs_recv.at[p, 3], down)
        for j in range(4):
            rs[p, j].start()

    def stage_d(p):
        rs[p, 0].wait_recv()
        part[p, lo, 3] = (part[p, lo, 3].astype(F32) + ring_a[p, 0].astype(F32)).astype(BF)
        rs[p, 4] = remote(part.at[p, lo, 3], ring_b.at[p, lo], rs_send.at[p, 4], rs_recv.at[p, 4], up)
        rs[p, 4].start()
        rs[p, 1].wait_recv()
        part[p, hi, 1] = (part[p, hi, 1].astype(F32) + ring_a[p, 1].astype(F32)).astype(BF)
        rs[p, 5] = remote(part.at[p, hi, 1], ring_c.at[p, hi], rs_send.at[p, 5], rs_recv.at[p, 5], down)
        rs[p, 5].start()

    def stage_e(p):
        for j in range(2, 6):
            rs[p, j].wait_recv()
        total = part[p, :, 0].astype(F32) + ring_b[p].astype(F32) + ring_c[p].astype(F32)
        ret[pl.ds(256 * p, 256), :] = dot(perm[...], total.astype(BF).reshape(256, HALF)).astype(BF)

        def post(k, _):
            pltpu.make_async_remote_copy(
                src_ref=ret.at[pl.ds(pl.multiple_of(k * 16, 16), 16)],
                dst_ref=back.at[pl.ds(pl.multiple_of(me * 16, 16), 16)],
                send_sem=ret_send.at[0],
                recv_sem=ret_recv.at[0],
                device_id=plane(lax.rem(me + 64 - k, 64)),
                device_id_type=MESH,
            ).start()
            return _

        lax.fori_loop(max(16 * p, 1), 16 * p + 16, post, 0)
        if p == 0:
            pltpu.make_async_copy(
                ret.at[pl.ds(0, 16)], back.at[pl.ds(pl.multiple_of(me * 16, 16), 16)], own_sem.at[1]
            ).start()

    def grad_first(h):
        total = None
        for p in range(PH):
            term = dot_tn(gath[p, 2 * h].reshape(256, HALF), hid[pl.ds(256 * p, 256), :])
            total = term if total is None else total + term
        ginv[pl.ds(h * HALF, HALF), :] = total.astype(BF)

    def grad_second(h):
        total = None
        for p in range(PH):
            term = dot_tn(act[pl.ds(256 * p, 256), :], gath[p, 2 * h + 1].reshape(256, HALF))
            total = term if total is None else total + term
        goutv[:, pl.ds(h * HALF, HALF)] = total.astype(BF)

    stage_a(0)
    stage_a(1)
    stage_b(0)
    stage_a(2)
    stage_b(1)
    stage_c(0)
    stage_a(3)
    stage_b(2)
    stage_c(1)
    stage_d(0)
    stage_b(3)
    stage_c(2)
    stage_d(1)
    stage_e(0)
    stage_c(3)
    stage_d(2)
    stage_e(1)
    grad_first(0)
    grad_first(1)
    out_gi = pltpu.make_async_copy(ginv, gi_h, out_sem.at[0])
    out_gi.start()
    stage_d(3)
    stage_e(2)
    grad_second(0)
    grad_second(1)
    out_go = pltpu.make_async_copy(goutv, go_h, out_sem.at[1])
    out_go.start()
    stage_e(3)

    pltpu.make_async_copy(
        ret.at[pl.ds(0, 16)], back.at[pl.ds(pl.multiple_of(me * 16, 16), 16)], own_sem.at[1]
    ).wait()
    wait_bytes(back.at[pl.ds(0, 63 * 16)], ret_recv.at[0])
    for g in range(4):
        rows = dot(perm_t[...], back[pl.ds(g * 256, 256), :]).astype(BF)
        for j in range(8):
            low[j, pl.ds(g * 32, 32), :] = rows[j * 32 : j * 32 + 32, :]
    logit = []
    turned = []
    for i in range(2):
        rows = pl.ds(i * 256, 256)
        h0, h1 = pl.ds(0, HALF), pl.ds(HALF, HALF)
        left = dot_nt(cot[rows, h0], low[i]) + dot_nt(cot[rows, h1], low[4 + i])
        right = dot_nt(tok[rows, h0], low[2 + i]) + dot_nt(tok[rows, h1], low[6 + i])
        c, d = comb[rows, :], disp[rows, :]
        g = c * (left - jnp.sum(c * left, axis=1, keepdims=True))
        g = g + d * (right - jnp.sum(d * right, axis=0, keepdims=True))
        logit.append(g.astype(BF))
        turned.append(g.astype(BF).T)
    for j in range(5):
        cols = pl.ds(j * 256, 256)
        term = dot(turned[0], tok[pl.ds(0, 256), cols]) + dot(turned[1], tok[pl.ds(256, 256), cols])
        rloc[cols, :] = term.T

    sibling = {"narrow": narrow + 1 - 2 * core}
    keep = pl.ds(pl.multiple_of(core * HALF, HALF), HALF)
    give = pl.ds(pl.multiple_of((1 - core) * HALF, HALF), HALF)
    first = remote(rloc.at[give], ar0, ar_send.at[0], ar_recv.at[0], sibling)
    first.start()

    def image_out(i):
        rows = pl.ds(i * 256, 256)
        dl = disp[rows, :].astype(BF)
        cl = comb[rows, :].astype(BF)
        for h in range(2):
            cols = pl.ds(h * HALF, HALF)
            mixed[rows, cols] = dot(cl, low[h * 4 + i]).astype(BF)
            tgrad[rows, cols] = (
                dot(dl, low[h * 4 + 2 + i]) + dot_nt(logit[i], rout[cols, :])
            ).astype(BF)

    first.wait_recv()
    half[...] = rloc[keep, :] + ar0[...]

    def scatter(j, _):
        q = lax.rem(spot + j, 16)
        remote(
            half.at[pl.ds(pl.multiple_of(q * 40, 8), 40)], ar1.at[j],
            ar_send.at[1], ar_recv.at[1], chip(q),
        ).start()
        return _

    lax.fori_loop(1, 16, scatter, 0)
    image_out(0)
    wait_bytes(ar1.at[pl.ds(1, 15)], ar_recv.at[1])
    total = half[pl.ds(pl.multiple_of(spot * 40, 8), 40), :]
    for j in range(1, 16):
        total = total + ar1[j]
    one[...] = total
    ar2[z] = total

    def across(j, _):
        to = (wide // 8) * 8 + lax.rem(z + j, 8)
        remote(one, ar2.at[z], ar_send.at[2], ar_recv.at[2], {"wide": to}).start()
        return _

    lax.fori_loop(1, 8, across, 0)
    image_out(1)
    out_mixed = pltpu.make_async_copy(mixed, mixed_h, out_sem.at[2])
    out_mixed.start()
    out_tg = pltpu.make_async_copy(tgrad, tg_h, out_sem.at[3])
    out_tg.start()
    wait_bytes(ar2.at[pl.ds(0, 7)], ar_recv.at[2])
    total = ar2[0]
    for j in range(1, 8):
        total = total + ar2[j]
    place = pl.ds(pl.multiple_of(core * HALF + spot * 40, 8), 40)
    fin[place, :] = total

    def spread(j, _):
        q = lax.rem(spot + j, 16)
        remote(fin.at[place], fin.at[place], ar_send.at[3], ar_recv.at[3], chip(q)).start()
        return _

    lax.fori_loop(1, 16, spread, 0)
    wait_bytes(ar1.at[pl.ds(1, 15)], ar_recv.at[3])
    last = remote(fin.at[keep], fin.at[keep], ar_send.at[4], ar_recv.at[4], sibling)
    last.start()
    last.wait_recv()
    out_rg = pltpu.make_async_copy(fin, rg_h, out_sem.at[4])
    out_rg.start()

    wait_bytes(recv.at[pl.ds(0, 63 * 16)], a2a_send.at[0])
    wait_bytes(recv.at[pl.ds(0, 63 * 16)], ret_send.at[0])
    for c in list(ag.values()) + list(rs.values()):
        c.wait_send()
    first.wait_send()
    last.wait_send()
    wait_bytes(ar1.at[pl.ds(1, 15)], ar_send.at[1])
    wait_bytes(ar2.at[pl.ds(0, 7)], ar_send.at[2])
    wait_bytes(ar1.at[pl.ds(1, 15)], ar_send.at[3])
    for c in (out_gi, out_go, out_mixed, out_tg, out_rg):
        c.wait()


def local(tokens, router, expert_in, expert_out, cotangent):
    images, length, width = tokens.shape
    slots = router.shape[1]
    hidden = expert_in.shape[2]
    rows = images * length
    vm = pltpu.VMEM
    dma = pltpu.SemaphoreType.DMA
    anywhere = pl.BlockSpec(memory_space=pl.ANY)
    out = pl.pallas_call(
        kernel,
        out_shape=(
            jax.ShapeDtypeStruct((rows, width), BF),
            jax.ShapeDtypeStruct((rows, width), BF),
            jax.ShapeDtypeStruct((width, slots), F32),
            jax.ShapeDtypeStruct((width, hidden), BF),
            jax.ShapeDtypeStruct((hidden, width), BF),
        ),
        in_specs=[anywhere] * 5,
        out_specs=[anywhere] * 5,
        scratch_shapes=[
            vm((rows, width), BF), vm((width, slots), BF), vm((width, hidden), BF),
            vm((hidden, width), BF), vm((rows, width), BF),
            vm((256, 256), BF), vm((256, 256), BF),
            vm((rows, slots), F32), vm((rows, slots), F32),
            vm((4, 256, HALF), BF), vm((1024, HALF), BF), vm((1024, HALF), BF),
            vm((PH, 4, 4, 64, HALF), BF), vm((PH, 4, 4, 64, HALF), BF),
            vm((PH, 2, 2, 64, HALF), BF),
            vm((PH, 4, 64, HALF), BF), vm((PH, 4, 64, HALF), BF),
            vm((256, hidden), F32), vm((256, hidden), F32),
            vm((1024, hidden), BF), vm((1024, hidden), BF),
            vm((1024, HALF), BF), vm((1024, HALF), BF),
            vm((8, 128, HALF), BF),
            vm((rows, width), BF), vm((rows, width), BF),
            vm((width, hidden), BF), vm((hidden, width), BF),
            vm((width, slots), F32), vm((HALF, slots), F32), vm((HALF, slots), F32),
            vm((16, 40, slots), F32), vm((8, 40, slots), F32), vm((40, slots), F32),
            vm((width, slots), F32),
            dma((5,)), dma((5,)), dma((2,)), dma((1,)), dma((PH,)),
            dma((PH, 4)), dma((PH, 4)), dma((PH, 6)), dma((PH, 6)),
            dma((1,)), dma((1,)), dma((5,)), dma((5,)),
        ],
        compiler_params=pltpu.CompilerParams(
            collective_id=0, has_side_effects=True, vmem_limit_bytes=60 * 1024 * 1024
        ),
        cost_estimate=pl.CostEstimate(
            flops=12 * 10**9, bytes_accessed=12 * 10**6, transcendentals=2 * 10**6
        ),
    )(
        tokens.reshape(rows, width), router, expert_in[0], expert_out[0],
        cotangent.reshape(rows, width),
    )
    mixed, token_grad, router_grad, grad_in, grad_out = out
    return (
        mixed.reshape(images, length, width),
        token_grad.reshape(images, length, width),
        router_grad,
        grad_in[None],
        grad_out[None],
    )


def solution(mesh):
    in_specs = (
        P(("dp", "wide", "narrow"), None, None),
        P(),
        P(("wide", "narrow"), None, "dp"),
        P(("wide", "narrow"), "dp", None),
        P(("dp", "wide", "narrow"), None, None),
    )
    out_specs = (
        P(("dp", "wide", "narrow"), None, None),
        P(("dp", "wide", "narrow"), None, None),
        P(),
        P(("wide", "narrow"), None, "dp"),
        P(("wide", "narrow"), "dp", None),
    )
    return jax.shard_map(local, mesh=mesh, in_specs=in_specs, out_specs=out_specs, check_vma=False)
```

```python
import functools

import jax
import jax.numpy as jnp
from jax import lax
from jax.experimental import pallas as pl
from jax.experimental.pallas import tpu as pltpu
from jax.sharding import PartitionSpec as P

MESH = pl.DeviceIdType.MESH
BF = jnp.bfloat16
F32 = jnp.float32
PH = 8
MSG = 64 // PH
ROWS = 16 * MSG
EACH = ROWS // 4
CHAINS = ((0, 24), (24, 16))
HALF = 640


def dot(a, b):
    return jnp.dot(a, b, preferred_element_type=F32)


def dot_nt(a, b):
    return lax.dot_general(a, b, (((1,), (1,)), ((), ())), preferred_element_type=F32)


def dot_tn(a, b):
    return lax.dot_general(a, b, (((0,), (0,)), ((), ())), preferred_element_type=F32)


def normal_cdf_pdf(x):
    z = jnp.abs(x) * 0.7071067811865476
    t = 1.0 / (1.0 + 0.5 * z)
    poly = 0.17087277
    for c in (
        -0.82215223,
        1.48851587,
        -1.13520398,
        0.27886807,
        -0.18628806,
        0.09678418,
        0.37409196,
        1.00002368,
        -1.26551223,
    ):
        poly = poly * t + c
    square = z * z
    tail = 0.5 * t * jnp.exp(poly - square)
    cdf = jnp.where(x < 0, tail, 1.0 - tail)
    pdf = 0.3989422804014327 * jnp.exp(-square)
    return cdf, pdf


def kernel(
    tok_h, rout_h, win_h, wout_h, cot_h,
    mixed, tgrad, fin, ginv, goutv,
    tok, rout, win, wout, cot,
    perm, perm_t, disp, comb, stage, send, recv, gath, part, ring_a, ring_b, ring_c,
    pre, back_f, act, hid, ret, back, low,
    give_v, keep_v, ar0_a, ar0_b, half_a, half_b, ar1_a, ar1_b, one_a, one_b, ar2_a, ar2_b,
    load_sem, own_sem, a2a_send, a2a_recv, ag_send, ag_recv, rs_send, rs_recv,
    ret_send, ret_recv, ar_send, ar_recv,
):
    y = lax.axis_index("dp")
    wide = lax.axis_index("wide")
    narrow = lax.axis_index("narrow")
    me = wide * 4 + narrow
    z = lax.rem(wide, 8)
    x = (wide // 8) * 2 + narrow // 2
    core = lax.rem(narrow, 2)
    spot = y * 4 + x

    def plane(e):
        return {"wide": e // 4, "narrow": lax.rem(e, 4)}

    def place_of(k, sign):
        j = k % 8
        dz = (j % 2) * ((j + 1) // 2) + (1 - j % 2) * (8 - j // 2)
        px = (x + sign * (k // 16) + 4) % 4
        pz = (z + sign * dz + 8) % 8
        pc = (core + k // 8) % 2
        return (px // 2) * 8 + pz, (px % 2) * 2 + pc

    def chip(q):
        cx = lax.rem(q, 4)
        return {"dp": q // 4, "wide": (cx // 2) * 8 + z, "narrow": lax.rem(cx, 2) * 2 + core}

    up = {"dp": lax.rem(y + 1, 4)}
    down = {"dp": lax.rem(y + 3, 4)}

    loads = [
        pltpu.make_async_copy(a, b, load_sem.at[i])
        for i, (a, b) in enumerate(
            ((tok_h, tok), (rout_h, rout), (cot_h, cot), (win_h, win), (wout_h, wout))
        )
    ]
    for c in loads:
        c.start()

    barrier = pltpu.get_barrier_semaphore()

    def greet(k, _):
        pl.semaphore_signal(
            barrier, inc=1, device_id=plane(lax.rem(me + k, 64)), device_id_type=MESH
        )
        return _

    lax.fori_loop(1, 64, greet, 0)

    def greet_far(k, _):
        q = lax.rem(y + 1 + k // 4, 4) * 4 + lax.rem(k, 4)
        pl.semaphore_signal(barrier, inc=1, device_id=chip(q), device_id_type=MESH)
        return _

    lax.fori_loop(0, 12, greet_far, 0)

    def source(r):
        e = r // 16
        h = (r // 8) % 2
        c = (r // 4) % 2
        s = (r // 2) % 2
        return (h * 4 + c * 2 + r % 2) * EACH // 2 + e * 2 + s

    i0 = lax.broadcasted_iota(jnp.int32, (ROWS, ROWS), 0)
    i1 = lax.broadcasted_iota(jnp.int32, (ROWS, ROWS), 1)
    perm[...] = jnp.where(source(i0) == i1, 1.0, 0.0).astype(BF)
    perm_t[...] = jnp.where(source(i1) == i0, 1.0, 0.0).astype(BF)

    loads[0].wait()
    loads[1].wait()
    for i in range(2):
        rows = pl.ds(i * 256, 256)
        logits = dot(tok[rows, :], rout[...])
        d = jnp.exp(logits - jnp.max(logits, axis=0, keepdims=True))
        d = d / jnp.sum(d, axis=0, keepdims=True)
        c = jnp.exp(logits - jnp.max(logits, axis=1, keepdims=True))
        c = c / jnp.sum(c, axis=1, keepdims=True)
        disp[rows, :] = d
        comb[rows, :] = c
        if i == 0:
            loads[2].wait()
        for kind, (weight, values) in enumerate(((d, tok), (c, cot))):
            weight_t = weight.astype(BF).T
            for h in range(2):
                slots = dot(weight_t, values[rows, pl.ds(h * HALF, HALF)]).astype(BF)
                for g in range(PH):
                    stage[g, pl.ds((h * 4 + kind * 2 + i) * EACH // 2, EACH // 2), :] = slots[
                        g * EACH // 2 : (g + 1) * EACH // 2, :
                    ]
    for g in range(PH):
        send[pl.ds(g * ROWS, ROWS), :] = dot(perm[...], stage[g]).astype(BF)

    pl.semaphore_wait(barrier, 75)

    own = pltpu.make_async_copy(
        send.at[pl.ds(pl.multiple_of(me * 16, 16), 16)], recv.at[pl.ds(0, 16)], own_sem.at[0]
    )
    own.start()
    for p in range(PH):

        def post(k, _, p=p):
            w, n = place_of(k, 1)
            pltpu.make_async_remote_copy(
                src_ref=send.at[pl.ds(pl.multiple_of((w * 4 + n) * 16, 16), 16)],
                dst_ref=recv.at[pl.ds(pl.multiple_of(k * 16, 16), 16)],
                send_sem=a2a_send.at[0],
                recv_sem=a2a_recv.at[p],
                device_id={"wide": w, "narrow": n},
                device_id_type=MESH,
            ).start()
            return _

        lax.fori_loop(max(MSG * p, 1), MSG * p + MSG, post, 0)

    def wait_bytes(ref, sem):
        pltpu.make_async_copy(ref, ref, sem).wait()

    def remote(src, dst, s, r, to):
        return pltpu.make_async_remote_copy(
            src_ref=src, dst_ref=dst, send_sem=s, recv_sem=r, device_id=to, device_id_type=MESH
        )

    lo, hi = pl.ds(0, 2), pl.ds(2, 2)
    ag = {}
    rs = {}

    def stage_a(p):
        if p == 0:
            own.wait()
            wait_bytes(recv.at[pl.ds(16, ROWS - 16)], a2a_recv.at[0])
        else:
            wait_bytes(recv.at[pl.ds(ROWS * p, ROWS)], a2a_recv.at[p])
        rows = dot(perm_t[...], recv[pl.ds(ROWS * p, ROWS), :]).astype(BF)
        gath[p, :, 0] = rows.reshape(4, EACH, HALF)
        ag[p, 0] = remote(gath.at[p, :, 0], gath.at[p, :, 1], ag_send.at[p, 0], ag_recv.at[p, 0], up)
        ag[p, 1] = remote(gath.at[p, :, 0], gath.at[p, :, 3], ag_send.at[p, 1], ag_recv.at[p, 1], down)
        ag[p, 0].start()
        ag[p, 1].start()

    def stage_b(p):
        ag[p, 0].wait_recv()
        ag[p, 2] = remote(gath.at[p, lo, 1], gath.at[p, lo, 2], ag_send.at[p, 2], ag_recv.at[p, 2], up)
        ag[p, 2].start()
        ag[p, 1].wait_recv()
        ag[p, 3] = remote(gath.at[p, hi, 3], gath.at[p, hi, 2], ag_send.at[p, 3], ag_recv.at[p, 3], down)
        ag[p, 3].start()

    def stage_c(p):
        ag[p, 2].wait_recv()
        ag[p, 3].wait_recv()
        if p == 0:
            loads[3].wait()
            loads[4].wait()
        mine = pl.ds(4 * EACH * p, 4 * EACH)

        def rows(q):
            return gath[p, q].reshape(4 * EACH, HALF)

        pre[...] = dot(rows(0), win[pl.ds(0, HALF), :]) + dot(rows(2), win[pl.ds(HALF, HALF), :])
        back_f[...] = dot_nt(rows(1), wout[:, pl.ds(0, HALF)]) + dot_nt(
            rows(3), wout[:, pl.ds(HALF, HALF)]
        )

        def nonlinear(j, _):
            r = pl.ds(pl.multiple_of(j * 16, 16), 16)
            v = pre[r, :]
            cdf, pdf = normal_cdf_pdf(v)
            to = pl.ds(pl.multiple_of(4 * EACH * p + j * 16, 16), 16)
            act[to, :] = (v * cdf).astype(BF)
            hid[to, :] = (back_f[r, :] * (cdf + v * pdf)).astype(BF)
            return _

        lax.fori_loop(0, EACH // 4, nonlinear, 0)
        for h in range(2):
            cols = pl.ds(h * HALF, HALF)
            part[p, 2 * h] = dot(act[mine, :], wout[:, cols]).astype(BF).reshape(4, EACH, HALF)
            part[p, 2 * h + 1] = dot_nt(hid[mine, :], win[cols, :]).astype(BF).reshape(4, EACH, HALF)
        rs[p, 0] = remote(part.at[p, lo, 2], ring_a.at[p, 0], rs_send.at[p, 0], rs_recv.at[p, 0], up)
        rs[p, 1] = remote(part.at[p, hi, 2], ring_a.at[p, 1], rs_send.at[p, 1], rs_recv.at[p, 1], down)
        rs[p, 2] = remote(part.at[p, hi, 3], ring_b.at[p, hi], rs_send.at[p, 2], rs_recv.at[p, 2], up)
        rs[p, 3] = remote(part.at[p, lo, 1], ring_c.at[p, lo], rs_send.at[p, 3], rs_recv.at[p, 3], down)
        for j in range(4):
            rs[p, j].start()

    def stage_d(p):
        rs[p, 0].wait_recv()
        part[p, lo, 3] = (part[p, lo, 3].astype(F32) + ring_a[p, 0].astype(F32)).astype(BF)
        rs[p, 4] = remote(part.at[p, lo, 3], ring_b.at[p, lo], rs_send.at[p, 4], rs_recv.at[p, 4], up)
        rs[p, 4].start()
        rs[p, 1].wait_recv()
        part[p, hi, 1] = (part[p, hi, 1].astype(F32) + ring_a[p, 1].astype(F32)).astype(BF)
        rs[p, 5] = remote(part.at[p, hi, 1], ring_c.at[p, hi], rs_send.at[p, 5], rs_recv.at[p, 5], down)
        rs[p, 5].start()

    def stage_e(p):
        for j in range(2, 6):
            rs[p, j].wait_recv()
        total = part[p, :, 0].astype(F32) + ring_b[p].astype(F32) + ring_c[p].astype(F32)
        ret[pl.ds(ROWS * p, ROWS), :] = dot(perm[...], total.astype(BF).reshape(ROWS, HALF)).astype(BF)

        def post(k, _):
            w, n = place_of(k, -1)
            pltpu.make_async_remote_copy(
                src_ref=ret.at[pl.ds(pl.multiple_of(k * 16, 16), 16)],
                dst_ref=back.at[pl.ds(pl.multiple_of(me * 16, 16), 16)],
                send_sem=ret_send.at[0],
                recv_sem=ret_recv.at[0],
                device_id={"wide": w, "narrow": n},
                device_id_type=MESH,
            ).start()
            return _

        lax.fori_loop(max(MSG * p, 1), MSG * p + MSG, post, 0)
        if p == 0:
            pltpu.make_async_copy(
                ret.at[pl.ds(0, 16)], back.at[pl.ds(pl.multiple_of(me * 16, 16), 16)], own_sem.at[1]
            ).start()

    def grad_first(h):
        total = None
        for p in range(PH):
            term = dot_tn(
                gath[p, 2 * h].reshape(4 * EACH, HALF), hid[pl.ds(4 * EACH * p, 4 * EACH), :]
            )
            total = term if total is None else total + term
        ginv[pl.ds(h * HALF, HALF), :] = total.astype(BF)

    def grad_second(h):
        total = None
        for p in range(PH):
            term = dot_tn(
                act[pl.ds(4 * EACH * p, 4 * EACH), :], gath[p, 2 * h + 1].reshape(4 * EACH, HALF)
            )
            total = term if total is None else total + term
        goutv[:, pl.ds(h * HALF, HALF)] = total.astype(BF)

    for t in range(PH + 4):
        if t < PH:
            stage_a(t)
        if 0 <= t - 1 < PH:
            stage_b(t - 1)
        if 0 <= t - 2 < PH:
            stage_c(t - 2)
        if 0 <= t - 3 < PH:
            stage_d(t - 3)
        if t == PH + 2:
            grad_first(0)
            grad_first(1)
        if 0 <= t - 4 < PH:
            stage_e(t - 4)
    grad_second(0)
    grad_second(1)

    pltpu.make_async_copy(
        ret.at[pl.ds(0, 16)], back.at[pl.ds(pl.multiple_of(me * 16, 16), 16)], own_sem.at[1]
    ).wait()
    wait_bytes(back.at[pl.ds(0, 63 * 16)], ret_recv.at[0])
    for g in range(PH):
        rows = dot(perm_t[...], back[pl.ds(g * ROWS, ROWS), :]).astype(BF)
        for j in range(8):
            low[j, pl.ds(g * EACH // 2, EACH // 2), :] = rows[j * EACH // 2 : (j + 1) * EACH // 2, :]
    logit = []
    turned = []
    for i in range(2):
        rows = pl.ds(i * 256, 256)
        h0, h1 = pl.ds(0, HALF), pl.ds(HALF, HALF)
        left = dot_nt(cot[rows, h0], low[i]) + dot_nt(cot[rows, h1], low[4 + i])
        right = dot_nt(tok[rows, h0], low[2 + i]) + dot_nt(tok[rows, h1], low[6 + i])
        c, d = comb[rows, :], disp[rows, :]
        g = c * (left - jnp.sum(c * left, axis=1, keepdims=True))
        g = g + d * (right - jnp.sum(d * right, axis=0, keepdims=True))
        logit.append(g.astype(BF))
        turned.append(g.astype(BF).T)

    def router_half(which):
        cols = pl.ds(pl.multiple_of(which * HALF, HALF), HALF)
        term = dot(turned[0], tok[pl.ds(0, 256), cols]) + dot(turned[1], tok[pl.ds(256, 256), cols])
        return term.T.reshape(16, 40, 128)

    sibling = {"narrow": narrow + 1 - 2 * core}
    chains = [
        (c, pl.ds(off, n), n, *refs)
        for c, ((off, n), refs) in enumerate(
            zip(
                CHAINS,
                ((ar0_a, half_a, ar1_a, one_a, ar2_a), (ar0_b, half_b, ar1_b, one_b, ar2_b)),
            )
        )
    ]
    give_v[...] = router_half(1 - core)
    first = []
    for c, span, n, ar0, half, ar1, one, ar2 in chains:
        first.append(
            remote(give_v.at[:, span], ar0, ar_send.at[0, c], ar_recv.at[0, c], sibling)
        )
        first[-1].start()
    keep_v[...] = router_half(core)

    def image_out(i):
        rows = pl.ds(i * 256, 256)
        dl = disp[rows, :].astype(BF)
        cl = comb[rows, :].astype(BF)
        for h in range(2):
            cols = pl.ds(h * HALF, HALF)
            mixed[rows, cols] = dot(cl, low[h * 4 + i]).astype(BF)
            tgrad[rows, cols] = (
                dot(dl, low[h * 4 + 2 + i]) + dot_nt(logit[i], rout[cols, :])
            ).astype(BF)

    for c, span, n, ar0, half, ar1, one, ar2 in chains:
        first[c].wait_recv()
        half[...] = keep_v[:, span, :] + ar0[...]

        def scatter(j, _, c=c, half=half, ar1=ar1):
            q = lax.rem(spot + j, 16)
            remote(half.at[q], ar1.at[j], ar_send.at[1, c], ar_recv.at[1, c], chip(q)).start()
            return _

        lax.fori_loop(1, 16, scatter, 0)
    image_out(0)
    for c, span, n, ar0, half, ar1, one, ar2 in chains:
        wait_bytes(ar1.at[pl.ds(1, 15)], ar_recv.at[1, c])
        total = half[spot]
        for j in range(1, 16):
            total = total + ar1[j]
        one[...] = total
        ar2[z] = total

        def across(j, _, c=c, one=one, ar2=ar2):
            to = (wide // 8) * 8 + lax.rem(z + j, 8)
            remote(one, ar2.at[z], ar_send.at[2, c], ar_recv.at[2, c], {"wide": to}).start()
            return _

        lax.fori_loop(1, 8, across, 0)
    image_out(1)
    for c, span, n, ar0, half, ar1, one, ar2 in chains:
        wait_bytes(ar2.at[pl.ds(0, 7)], ar_recv.at[2, c])
        total = ar2[0]
        for j in range(1, 8):
            total = total + ar2[j]
        fin[core, spot, span, :] = total

        def spread(j, _, c=c, span=span):
            mine = fin.at[core, spot, span]
            remote(
                mine, mine, ar_send.at[3, c], ar_recv.at[3, c], chip(lax.rem(spot + j, 16))
            ).start()
            return _

        lax.fori_loop(1, 16, spread, 0)
    last = []
    for c, span, n, ar0, half, ar1, one, ar2 in chains:
        wait_bytes(ar1.at[pl.ds(1, 15)], ar_recv.at[3, c])
        done = fin.at[core, :, span]
        last.append(remote(done, done, ar_send.at[4, c], ar_recv.at[4, c], sibling))
        last[-1].start()
    for c in last:
        c.wait_recv()

    wait_bytes(recv.at[pl.ds(0, 63 * 16)], a2a_send.at[0])
    wait_bytes(recv.at[pl.ds(0, 63 * 16)], ret_send.at[0])
    for c in list(ag.values()) + list(rs.values()):
        c.wait_send()
    for c in first + last:
        c.wait_send()
    for c, span, n, ar0, half, ar1, one, ar2 in chains:
        wait_bytes(ar1.at[pl.ds(1, 15)], ar_send.at[1, c])
        wait_bytes(ar2.at[pl.ds(0, 7)], ar_send.at[2, c])
        wait_bytes(ar1.at[pl.ds(1, 15)], ar_send.at[3, c])


def write_out(*refs):
    sem = refs[-1]
    copies = [pltpu.make_async_copy(refs[i], refs[5 + i], sem.at[i]) for i in range(5)]
    for c in copies:
        c.start()
    for c in copies:
        c.wait()


def local(tokens, router, expert_in, expert_out, cotangent):
    images, length, width = tokens.shape
    slots = router.shape[1]
    hidden = expert_in.shape[2]
    rows = images * length
    vm = pltpu.VMEM
    dma = pltpu.SemaphoreType.DMA
    anywhere = pl.BlockSpec(memory_space=pl.ANY)
    outs = (
        jax.ShapeDtypeStruct((rows, width), BF),
        jax.ShapeDtypeStruct((rows, width), BF),
        jax.ShapeDtypeStruct((2, 16, 40, slots), F32),
        jax.ShapeDtypeStruct((width, hidden), BF),
        jax.ShapeDtypeStruct((hidden, width), BF),
    )
    out = pl.pallas_call(
        kernel,
        out_shape=tuple(pltpu.VMEM(o.shape, o.dtype) for o in outs),
        in_specs=[anywhere] * 5,
        out_specs=[pl.BlockSpec(memory_space=pltpu.VMEM)] * 5,
        scratch_shapes=[
            vm((rows, width), BF), vm((width, slots), BF), vm((width, hidden), BF),
            vm((hidden, width), BF), vm((rows, width), BF),
            vm((ROWS, ROWS), BF), vm((ROWS, ROWS), BF),
            vm((rows, slots), F32), vm((rows, slots), F32),
            vm((PH, ROWS, HALF), BF), vm((1024, HALF), BF), vm((1024, HALF), BF),
            vm((PH, 4, 4, EACH, HALF), BF), vm((PH, 4, 4, EACH, HALF), BF),
            vm((PH, 2, 2, EACH, HALF), BF),
            vm((PH, 4, EACH, HALF), BF), vm((PH, 4, EACH, HALF), BF),
            vm((4 * EACH, hidden), F32), vm((4 * EACH, hidden), F32),
            vm((1024, hidden), BF), vm((1024, hidden), BF),
            vm((1024, HALF), BF), vm((1024, HALF), BF),
            vm((8, 128, HALF), BF),
            vm((16, 40, slots), F32), vm((16, 40, slots), F32),
            vm((16, 24, slots), F32), vm((16, 16, slots), F32),
            vm((16, 24, slots), F32), vm((16, 16, slots), F32),
            vm((16, 24, slots), F32), vm((16, 16, slots), F32),
            vm((24, slots), F32), vm((16, slots), F32),
            vm((8, 24, slots), F32), vm((8, 16, slots), F32),
            dma((5,)), dma((2,)), dma((1,)), dma((PH,)),
            dma((PH, 4)), dma((PH, 4)), dma((PH, 6)), dma((PH, 6)),
            dma((1,)), dma((1,)), dma((5, 2)), dma((5, 2)),
        ],
        compiler_params=pltpu.CompilerParams(
            collective_id=0, has_side_effects=True, vmem_limit_bytes=50 * 1024 * 1024
        ),
        cost_estimate=pl.CostEstimate(
            flops=12 * 10**9, bytes_accessed=12 * 10**6, transcendentals=2 * 10**6
        ),
    )(
        tokens.reshape(rows, width), router, expert_in[0], expert_out[0],
        cotangent.reshape(rows, width),
    )
    out = pl.pallas_call(
        write_out,
        out_shape=outs,
        in_specs=[pl.BlockSpec(memory_space=pltpu.VMEM)] * 5,
        out_specs=[anywhere] * 5,
        scratch_shapes=[dma((5,))],
    )(*out)
    mixed, token_grad, router_grad, grad_in, grad_out = out
    return (
        mixed.reshape(images, length, width),
        token_grad.reshape(images, length, width),
        router_grad.reshape(width, slots),
        grad_in[None],
        grad_out[None],
    )


def solution(mesh):
    in_specs = (
        P(("dp", "wide", "narrow"), None, None),
        P(),
        P(("wide", "narrow"), None, "dp"),
        P(("wide", "narrow"), "dp", None),
        P(("dp", "wide", "narrow"), None, None),
    )
    out_specs = (
        P(("dp", "wide", "narrow"), None, None),
        P(("dp", "wide", "narrow"), None, None),
        P(),
        P(("wide", "narrow"), None, "dp"),
        P(("wide", "narrow"), "dp", None),
    )
    return jax.shard_map(local, mesh=mesh, in_specs=in_specs, out_specs=out_specs, check_vma=False)
```

```python
import functools

import jax
import jax.numpy as jnp
from jax import lax
from jax.experimental import pallas as pl
from jax.experimental.pallas import tpu as pltpu
from jax.sharding import PartitionSpec as P

MESH = pl.DeviceIdType.MESH
BF = jnp.bfloat16
F32 = jnp.float32
PH = 8
MSG = 64 // PH
ROWS = 16 * MSG
EACH = ROWS // 4
STEPS = ((0, 0), (0, 1), (1, 0), (1, 1), (2, 0), (2, 1), (3, 0), (3, 1))
OWN = STEPS.index((0, 0)) * MSG
HALF = 640


def dot(a, b):
    return jnp.dot(a, b, preferred_element_type=F32)


def dot_nt(a, b):
    return lax.dot_general(a, b, (((1,), (1,)), ((), ())), preferred_element_type=F32)


def dot_tn(a, b):
    return lax.dot_general(a, b, (((0,), (0,)), ((), ())), preferred_element_type=F32)


def normal_cdf_pdf(x):
    z = jnp.abs(x) * 0.7071067811865476
    t = 1.0 / (1.0 + 0.5 * z)
    poly = 0.17087277
    for c in (
        -0.82215223,
        1.48851587,
        -1.13520398,
        0.27886807,
        -0.18628806,
        0.09678418,
        0.37409196,
        1.00002368,
        -1.26551223,
    ):
        poly = poly * t + c
    square = z * z
    tail = 0.5 * t * jnp.exp(poly - square)
    cdf = jnp.where(x < 0, tail, 1.0 - tail)
    pdf = 0.3989422804014327 * jnp.exp(-square)
    return cdf, pdf


def kernel(
    tok_h, rout_h, win_h, wout_h, cot_h,
    mixed, tgrad, fin, ginv, goutv,
    tok, rout, win, wout, cot,
    perm, perm_t, disp, comb, stage, send, recv, gath, part, ring_a, ring_b, ring_c,
    pre, back_f, act, hid, ret, back, low,
    give_v, keep_v, ar0, half, ar1, one, ar2, whole,
    load_sem, own_sem, a2a_send, a2a_recv, ag_send, ag_recv, rs_send, rs_recv,
    ret_send, ret_recv, ar_send, ar_recv,
):
    y = lax.axis_index("dp")
    wide = lax.axis_index("wide")
    narrow = lax.axis_index("narrow")
    me = wide * 4 + narrow
    z = lax.rem(wide, 8)
    x = (wide // 8) * 2 + narrow // 2
    core = lax.rem(narrow, 2)
    spot = y * 4 + x

    def plane(e):
        return {"wide": e // 4, "narrow": lax.rem(e, 4)}

    def place_of(p, k, sign):
        dx, dc = STEPS[p]
        j = lax.rem(k, 8)
        dz = (j % 2) * ((j + 1) // 2) + (1 - j % 2) * (8 - j // 2)
        px = (x + sign * dx + 4) % 4
        pz = (z + sign * dz + 8) % 8
        pc = (core + dc) % 2
        return (px // 2) * 8 + pz, (px % 2) * 2 + pc

    def chip(q):
        cx = lax.rem(q, 4)
        return {"dp": q // 4, "wide": (cx // 2) * 8 + z, "narrow": lax.rem(cx, 2) * 2 + core}

    up = {"dp": lax.rem(y + 1, 4)}
    down = {"dp": lax.rem(y + 3, 4)}

    loads = [
        pltpu.make_async_copy(a, b, load_sem.at[i])
        for i, (a, b) in enumerate(
            ((tok_h, tok), (rout_h, rout), (cot_h, cot), (win_h, win), (wout_h, wout))
        )
    ]
    for c in loads:
        c.start()

    barrier = pltpu.get_barrier_semaphore()

    def greet(k, _):
        pl.semaphore_signal(
            barrier, inc=1, device_id=plane(lax.rem(me + k, 64)), device_id_type=MESH
        )
        return _

    lax.fori_loop(1, 64, greet, 0)

    def greet_far(k, _):
        q = lax.rem(y + 1 + k // 4, 4) * 4 + lax.rem(k, 4)
        pl.semaphore_signal(barrier, inc=1, device_id=chip(q), device_id_type=MESH)
        return _

    lax.fori_loop(0, 12, greet_far, 0)

    give_v[:, pl.ds(40, 8), :] = jnp.zeros((16, 8, 128), F32)
    keep_v[:, pl.ds(40, 8), :] = jnp.zeros((16, 8, 128), F32)

    def source(r):
        e = r // 16
        h = (r // 8) % 2
        c = (r // 4) % 2
        s = (r // 2) % 2
        return (h * 4 + c * 2 + r % 2) * EACH // 2 + e * 2 + s

    i0 = lax.broadcasted_iota(jnp.int32, (ROWS, ROWS), 0)
    i1 = lax.broadcasted_iota(jnp.int32, (ROWS, ROWS), 1)
    perm[...] = jnp.where(source(i0) == i1, 1.0, 0.0).astype(BF)
    perm_t[...] = jnp.where(source(i1) == i0, 1.0, 0.0).astype(BF)

    loads[0].wait()
    loads[1].wait()
    for i in range(2):
        rows = pl.ds(i * 256, 256)
        logits = dot(tok[rows, :], rout[...])
        d = jnp.exp(logits - jnp.max(logits, axis=0, keepdims=True))
        d = d / jnp.sum(d, axis=0, keepdims=True)
        c = jnp.exp(logits - jnp.max(logits, axis=1, keepdims=True))
        c = c / jnp.sum(c, axis=1, keepdims=True)
        disp[rows, :] = d
        comb[rows, :] = c
        if i == 0:
            loads[2].wait()
        for kind, (weight, values) in enumerate(((d, tok), (c, cot))):
            weight_t = weight.astype(BF).T
            for h in range(2):
                slots = dot(weight_t, values[rows, pl.ds(h * HALF, HALF)]).astype(BF)
                for g in range(PH):
                    stage[g, pl.ds((h * 4 + kind * 2 + i) * EACH // 2, EACH // 2), :] = slots[
                        g * EACH // 2 : (g + 1) * EACH // 2, :
                    ]
    for g in range(PH):
        send[pl.ds(g * ROWS, ROWS), :] = dot(perm[...], stage[g]).astype(BF)

    pl.semaphore_wait(barrier, 75)

    own = pltpu.make_async_copy(
        send.at[pl.ds(pl.multiple_of(me * 16, 16), 16)], recv.at[pl.ds(16 * OWN, 16)], own_sem.at[0]
    )
    own.start()
    def post_phase(p):
        def post(k, _):
            w, n = place_of(p, k, 1)
            pltpu.make_async_remote_copy(
                src_ref=send.at[pl.ds(pl.multiple_of((w * 4 + n) * 16, 16), 16)],
                dst_ref=recv.at[pl.ds(pl.multiple_of(k * 16, 16), 16)],
                send_sem=a2a_send.at[0],
                recv_sem=a2a_recv.at[p],
                device_id={"wide": w, "narrow": n},
                device_id_type=MESH,
            ).start()
            return _

        lax.fori_loop(MSG * p + (STEPS[p] == (0, 0)), MSG * p + MSG, post, 0)

    for p in range(PH):
        post_phase(p)

    def wait_bytes(ref, sem):
        pltpu.make_async_copy(ref, ref, sem).wait()

    def remote(src, dst, s, r, to):
        return pltpu.make_async_remote_copy(
            src_ref=src, dst_ref=dst, send_sem=s, recv_sem=r, device_id=to, device_id_type=MESH
        )

    lo, hi = pl.ds(0, 2), pl.ds(2, 2)
    ag = {}
    rs = {}

    def stage_a(p):
        if STEPS[p] == (0, 0):
            own.wait()
            wait_bytes(recv.at[pl.ds(0, ROWS - 16)], a2a_recv.at[p])
        else:
            wait_bytes(recv.at[pl.ds(ROWS * p, ROWS)], a2a_recv.at[p])
        rows = dot(perm_t[...], recv[pl.ds(ROWS * p, ROWS), :]).astype(BF)
        gath[p, :, 0] = rows.reshape(4, EACH, HALF)
        ag[p, 0] = remote(gath.at[p, :, 0], gath.at[p, :, 1], ag_send.at[p, 0], ag_recv.at[p, 0], up)
        ag[p, 1] = remote(gath.at[p, :, 0], gath.at[p, :, 3], ag_send.at[p, 1], ag_recv.at[p, 1], down)
        ag[p, 0].start()
        ag[p, 1].start()

    def stage_b(p):
        ag[p, 0].wait_recv()
        ag[p, 2] = remote(gath.at[p, lo, 1], gath.at[p, lo, 2], ag_send.at[p, 2], ag_recv.at[p, 2], up)
        ag[p, 2].start()
        ag[p, 1].wait_recv()
        ag[p, 3] = remote(gath.at[p, hi, 3], gath.at[p, hi, 2], ag_send.at[p, 3], ag_recv.at[p, 3], down)
        ag[p, 3].start()

    def stage_c(p):
        ag[p, 2].wait_recv()
        ag[p, 3].wait_recv()
        if p == 0:
            loads[3].wait()
            loads[4].wait()
        mine = pl.ds(4 * EACH * p, 4 * EACH)

        def rows(q):
            return gath[p, q].reshape(4 * EACH, HALF)

        pre[...] = dot(rows(0), win[pl.ds(0, HALF), :]) + dot(rows(2), win[pl.ds(HALF, HALF), :])
        back_f[...] = dot_nt(rows(1), wout[:, pl.ds(0, HALF)]) + dot_nt(
            rows(3), wout[:, pl.ds(HALF, HALF)]
        )

        def nonlinear(j, _):
            r = pl.ds(pl.multiple_of(j * 16, 16), 16)
            v = pre[r, :]
            cdf, pdf = normal_cdf_pdf(v)
            to = pl.ds(pl.multiple_of(4 * EACH * p + j * 16, 16), 16)
            act[to, :] = (v * cdf).astype(BF)
            hid[to, :] = (back_f[r, :] * (cdf + v * pdf)).astype(BF)
            return _

        lax.fori_loop(0, EACH // 4, nonlinear, 0)
        for h in range(2):
            cols = pl.ds(h * HALF, HALF)
            part[p, 2 * h] = dot(act[mine, :], wout[:, cols]).astype(BF).reshape(4, EACH, HALF)
            part[p, 2 * h + 1] = dot_nt(hid[mine, :], win[cols, :]).astype(BF).reshape(4, EACH, HALF)
        rs[p, 0] = remote(part.at[p, lo, 2], ring_a.at[p, 0], rs_send.at[p, 0], rs_recv.at[p, 0], up)
        rs[p, 1] = remote(part.at[p, hi, 2], ring_a.at[p, 1], rs_send.at[p, 1], rs_recv.at[p, 1], down)
        rs[p, 2] = remote(part.at[p, hi, 3], ring_b.at[p, hi], rs_send.at[p, 2], rs_recv.at[p, 2], up)
        rs[p, 3] = remote(part.at[p, lo, 1], ring_c.at[p, lo], rs_send.at[p, 3], rs_recv.at[p, 3], down)
        for j in range(4):
            rs[p, j].start()

    def stage_d(p):
        rs[p, 0].wait_recv()
        part[p, lo, 3] = (part[p, lo, 3].astype(F32) + ring_a[p, 0].astype(F32)).astype(BF)
        rs[p, 4] = remote(part.at[p, lo, 3], ring_b.at[p, lo], rs_send.at[p, 4], rs_recv.at[p, 4], up)
        rs[p, 4].start()
        rs[p, 1].wait_recv()
        part[p, hi, 1] = (part[p, hi, 1].astype(F32) + ring_a[p, 1].astype(F32)).astype(BF)
        rs[p, 5] = remote(part.at[p, hi, 1], ring_c.at[p, hi], rs_send.at[p, 5], rs_recv.at[p, 5], down)
        rs[p, 5].start()

    def stage_e(p):
        for j in range(2, 6):
            rs[p, j].wait_recv()
        total = part[p, :, 0].astype(F32) + ring_b[p].astype(F32) + ring_c[p].astype(F32)
        ret[pl.ds(ROWS * p, ROWS), :] = dot(perm[...], total.astype(BF).reshape(ROWS, HALF)).astype(BF)

        def post(k, _):
            w, n = place_of(p, k, -1)
            pltpu.make_async_remote_copy(
                src_ref=ret.at[pl.ds(pl.multiple_of(k * 16, 16), 16)],
                dst_ref=back.at[pl.ds(pl.multiple_of(me * 16, 16), 16)],
                send_sem=ret_send.at[0],
                recv_sem=ret_recv.at[0],
                device_id={"wide": w, "narrow": n},
                device_id_type=MESH,
            ).start()
            return _

        lax.fori_loop(MSG * p + (STEPS[p] == (0, 0)), MSG * p + MSG, post, 0)
        if STEPS[p] == (0, 0):
            pltpu.make_async_copy(
                ret.at[pl.ds(16 * OWN, 16)], back.at[pl.ds(pl.multiple_of(me * 16, 16), 16)], own_sem.at[1]
            ).start()

    def grad_first(h):
        total = None
        for p in range(PH):
            term = dot_tn(
                gath[p, 2 * h].reshape(4 * EACH, HALF), hid[pl.ds(4 * EACH * p, 4 * EACH), :]
            )
            total = term if total is None else total + term
        ginv[pl.ds(h * HALF, HALF), :] = total.astype(BF)

    def grad_second(h):
        total = None
        for p in range(PH):
            term = dot_tn(
                act[pl.ds(4 * EACH * p, 4 * EACH), :], gath[p, 2 * h + 1].reshape(4 * EACH, HALF)
            )
            total = term if total is None else total + term
        goutv[:, pl.ds(h * HALF, HALF)] = total.astype(BF)

    for t in range(PH + 4):
        if t < PH:
            stage_a(t)
        if 0 <= t - 1 < PH:
            stage_b(t - 1)
        if 0 <= t - 2 < PH:
            stage_c(t - 2)
        if 0 <= t - 3 < PH:
            stage_d(t - 3)
        if 0 <= t - 4 < PH:
            stage_e(t - 4)
        if t == PH + 2:
            grad_first(0)
            grad_first(1)
    grad_second(0)
    grad_second(1)

    pltpu.make_async_copy(
        ret.at[pl.ds(16 * OWN, 16)], back.at[pl.ds(pl.multiple_of(me * 16, 16), 16)], own_sem.at[1]
    ).wait()
    wait_bytes(back.at[pl.ds(0, 63 * 16)], ret_recv.at[0])
    for g in range(PH):
        rows = dot(perm_t[...], back[pl.ds(g * ROWS, ROWS), :]).astype(BF)
        for j in range(8):
            low[j, pl.ds(g * EACH // 2, EACH // 2), :] = rows[j * EACH // 2 : (j + 1) * EACH // 2, :]
    logit = []
    turned = []
    for i in range(2):
        rows = pl.ds(i * 256, 256)
        h0, h1 = pl.ds(0, HALF), pl.ds(HALF, HALF)
        left = dot_nt(cot[rows, h0], low[i]) + dot_nt(cot[rows, h1], low[4 + i])
        right = dot_nt(tok[rows, h0], low[2 + i]) + dot_nt(tok[rows, h1], low[6 + i])
        c, d = comb[rows, :], disp[rows, :]
        g = c * (left - jnp.sum(c * left, axis=1, keepdims=True))
        g = g + d * (right - jnp.sum(d * right, axis=0, keepdims=True))
        logit.append(g.astype(BF))
        turned.append(g.astype(BF).T)

    def router_half(which):
        cols = pl.ds(pl.multiple_of(which * HALF, HALF), HALF)
        term = dot(turned[0], tok[pl.ds(0, 256), cols]) + dot(turned[1], tok[pl.ds(256, 256), cols])
        return term.T.reshape(16, 40, 128)

    sibling = {"narrow": narrow + 1 - 2 * core}
    give_v[:, pl.ds(0, 40), :] = router_half(1 - core)
    first = remote(give_v, ar0, ar_send.at[0], ar_recv.at[0], sibling)
    first.start()
    keep_v[:, pl.ds(0, 40), :] = router_half(core)

    def image_out(i):
        rows = pl.ds(i * 256, 256)
        dl = disp[rows, :].astype(BF)
        cl = comb[rows, :].astype(BF)
        for h in range(2):
            cols = pl.ds(h * HALF, HALF)
            mixed[rows, cols] = dot(cl, low[h * 4 + i]).astype(BF)
            tgrad[rows, cols] = (
                dot(dl, low[h * 4 + 2 + i]) + dot_nt(logit[i], rout[cols, :])
            ).astype(BF)

    first.wait_recv()
    half[...] = (keep_v[...] + ar0[...]).astype(BF)

    def scatter(j, _):
        q = lax.rem(spot + j, 16)
        remote(half.at[q], ar1.at[j], ar_send.at[1], ar_recv.at[1], chip(q)).start()
        return _

    lax.fori_loop(1, 16, scatter, 0)
    image_out(0)
    wait_bytes(ar1.at[pl.ds(1, 15)], ar_recv.at[1])
    total = half[spot].astype(F32)
    for j in range(1, 16):
        total = total + ar1[j].astype(F32)
    one[...] = total.astype(BF)
    ar2[z] = total.astype(BF)

    def across(j, _):
        to = (wide // 8) * 8 + lax.rem(z + j, 8)
        remote(one, ar2.at[z], ar_send.at[2], ar_recv.at[2], {"wide": to}).start()
        return _

    lax.fori_loop(1, 8, across, 0)
    image_out(1)
    wait_bytes(ar2.at[pl.ds(0, 7)], ar_recv.at[2])
    total = ar2[0].astype(F32)
    for j in range(1, 8):
        total = total + ar2[j].astype(F32)
    whole[core, spot] = total.astype(BF)

    def spread(j, _):
        mine = whole.at[core, spot]
        remote(mine, mine, ar_send.at[3], ar_recv.at[3], chip(lax.rem(spot + j, 16))).start()
        return _

    lax.fori_loop(1, 16, spread, 0)
    wait_bytes(ar1.at[pl.ds(1, 15)], ar_recv.at[3])
    last = remote(whole.at[core], whole.at[core], ar_send.at[4], ar_recv.at[4], sibling)
    last.start()
    fin[core] = whole[core].astype(F32)[:, :40, :]
    last.wait_recv()
    fin[1 - core] = whole[1 - core].astype(F32)[:, :40, :]

    wait_bytes(recv.at[pl.ds(0, 63 * 16)], a2a_send.at[0])
    wait_bytes(recv.at[pl.ds(0, 63 * 16)], ret_send.at[0])
    for c in list(ag.values()) + list(rs.values()):
        c.wait_send()
    first.wait_send()
    last.wait_send()
    wait_bytes(ar1.at[pl.ds(1, 15)], ar_send.at[1])
    wait_bytes(ar2.at[pl.ds(0, 7)], ar_send.at[2])
    wait_bytes(ar1.at[pl.ds(1, 15)], ar_send.at[3])


def write_out(*refs):
    sem = refs[-1]
    copies = [pltpu.make_async_copy(refs[i], refs[5 + i], sem.at[i]) for i in range(5)]
    for c in copies:
        c.start()
    for c in copies:
        c.wait()


def local(tokens, router, expert_in, expert_out, cotangent):
    images, length, width = tokens.shape
    slots = router.shape[1]
    hidden = expert_in.shape[2]
    rows = images * length
    vm = pltpu.VMEM
    dma = pltpu.SemaphoreType.DMA
    anywhere = pl.BlockSpec(memory_space=pl.ANY)
    outs = (
        jax.ShapeDtypeStruct((rows, width), BF),
        jax.ShapeDtypeStruct((rows, width), BF),
        jax.ShapeDtypeStruct((2, 16, 40, slots), F32),
        jax.ShapeDtypeStruct((width, hidden), BF),
        jax.ShapeDtypeStruct((hidden, width), BF),
    )
    out = pl.pallas_call(
        kernel,
        out_shape=tuple(pltpu.VMEM(o.shape, o.dtype) for o in outs),
        in_specs=[anywhere] * 5,
        out_specs=[pl.BlockSpec(memory_space=pltpu.VMEM)] * 5,
        scratch_shapes=[
            vm((rows, width), BF), vm((width, slots), BF), vm((width, hidden), BF),
            vm((hidden, width), BF), vm((rows, width), BF),
            vm((ROWS, ROWS), BF), vm((ROWS, ROWS), BF),
            vm((rows, slots), F32), vm((rows, slots), F32),
            vm((PH, ROWS, HALF), BF), vm((1024, HALF), BF), vm((1024, HALF), BF),
            vm((PH, 4, 4, EACH, HALF), BF), vm((PH, 4, 4, EACH, HALF), BF),
            vm((PH, 2, 2, EACH, HALF), BF),
            vm((PH, 4, EACH, HALF), BF), vm((PH, 4, EACH, HALF), BF),
            vm((4 * EACH, hidden), F32), vm((4 * EACH, hidden), F32),
            vm((1024, hidden), BF), vm((1024, hidden), BF),
            vm((1024, HALF), BF), vm((1024, HALF), BF),
            vm((8, 128, HALF), BF),
            vm((16, 48, slots), F32), vm((16, 48, slots), F32), vm((16, 48, slots), F32),
            vm((16, 48, slots), BF), vm((16, 48, slots), BF),
            vm((48, slots), BF), vm((8, 48, slots), BF), vm((2, 16, 48, slots), BF),
            dma((5,)), dma((2,)), dma((1,)), dma((PH,)),
            dma((PH, 4)), dma((PH, 4)), dma((PH, 6)), dma((PH, 6)),
            dma((1,)), dma((1,)), dma((5,)), dma((5,)),
        ],
        compiler_params=pltpu.CompilerParams(
            collective_id=0, has_side_effects=True, vmem_limit_bytes=50 * 1024 * 1024
        ),
        cost_estimate=pl.CostEstimate(
            flops=12 * 10**9, bytes_accessed=12 * 10**6, transcendentals=2 * 10**6
        ),
    )(
        tokens.reshape(rows, width), router, expert_in[0], expert_out[0],
        cotangent.reshape(rows, width),
    )
    out = pl.pallas_call(
        write_out,
        out_shape=outs,
        in_specs=[pl.BlockSpec(memory_space=pltpu.VMEM)] * 5,
        out_specs=[anywhere] * 5,
        scratch_shapes=[dma((5,))],
        compiler_params=pltpu.CompilerParams(vmem_limit_bytes=1024 * 1024),
    )(*out)
    mixed, token_grad, router_grad, grad_in, grad_out = out
    return (
        mixed.reshape(images, length, width),
        token_grad.reshape(images, length, width),
        router_grad.reshape(width, slots),
        grad_in[None],
        grad_out[None],
    )


def solution(mesh):
    in_specs = (
        P(("dp", "wide", "narrow"), None, None),
        P(),
        P(("wide", "narrow"), None, "dp"),
        P(("wide", "narrow"), "dp", None),
        P(("dp", "wide", "narrow"), None, None),
    )
    out_specs = (
        P(("dp", "wide", "narrow"), None, None),
        P(("dp", "wide", "narrow"), None, None),
        P(),
        P(("wide", "narrow"), None, "dp"),
        P(("wide", "narrow"), "dp", None),
    )
    return jax.shard_map(local, mesh=mesh, in_specs=in_specs, out_specs=out_specs, check_vma=False)
```

```python
import functools

import jax
import jax.numpy as jnp
from jax import lax
from jax.experimental import pallas as pl
from jax.experimental.pallas import tpu as pltpu
from jax.sharding import PartitionSpec as P

MESH = pl.DeviceIdType.MESH
BF = jnp.bfloat16
F32 = jnp.float32
PH = 8
MSG = 64 // PH
ROWS = 16 * MSG
EACH = ROWS // 4
STEPS = ((0, 0), (0, 1), (1, 0), (1, 1), (2, 0), (2, 1), (3, 0), (3, 1))
HALF = 640


def dot(a, b):
    return jnp.dot(a, b, preferred_element_type=F32)


def dot_nt(a, b):
    return lax.dot_general(a, b, (((1,), (1,)), ((), ())), preferred_element_type=F32)


def dot_tn(a, b):
    return lax.dot_general(a, b, (((0,), (0,)), ((), ())), preferred_element_type=F32)


def normal_cdf_pdf(x):
    z = jnp.abs(x) * 0.7071067811865476
    t = 1.0 / (1.0 + 0.5 * z)
    poly = 0.17087277
    for c in (
        -0.82215223,
        1.48851587,
        -1.13520398,
        0.27886807,
        -0.18628806,
        0.09678418,
        0.37409196,
        1.00002368,
        -1.26551223,
    ):
        poly = poly * t + c
    square = z * z
    tail = 0.5 * t * jnp.exp(poly - square)
    cdf = jnp.where(x < 0, tail, 1.0 - tail)
    pdf = 0.3989422804014327 * jnp.exp(-square)
    return cdf, pdf


def kernel(
    tok_h, rout_h, win_h, wout_h, cot_h,
    mixed, tgrad, fin, ginv, goutv,
    tok, rout, win, wout, cot,
    perm, perm_t, disp, comb, stage, send, recv, gath, part, ring_a, ring_b, ring_c,
    pre, back_f, act, hid, ret, back, low,
    early, spare, ret0, home, home_a, home_b, home_c,
    give_v, keep_v, ar0, half, ar1, one, ar2, whole,
    load_sem, own_sem, a2a_send, a2a_recv, ag_send, ag_recv, rs_send, rs_recv,
    ret_send, ret_recv, fwd_send, fwd_recv, home_send, home_recv, ar_send, ar_recv,
):
    y = lax.axis_index("dp")
    wide = lax.axis_index("wide")
    narrow = lax.axis_index("narrow")
    me = wide * 4 + narrow
    z = lax.rem(wide, 8)
    x = (wide // 8) * 2 + narrow // 2
    core = lax.rem(narrow, 2)
    spot = y * 4 + x

    def plane(e):
        return {"wide": e // 4, "narrow": lax.rem(e, 4)}

    def place_of(p, k, sign):
        dx, dc = STEPS[p]
        j = lax.rem(k, 8)
        dz = (j % 2) * ((j + 1) // 2) + (1 - j % 2) * (8 - j // 2)
        px = (x + sign * dx + 4) % 4
        pz = (z + sign * dz + 8) % 8
        pc = (core + dc) % 2
        return (px // 2) * 8 + pz, (px % 2) * 2 + pc

    def chip(q):
        cx = lax.rem(q, 4)
        return {"dp": q // 4, "wide": (cx // 2) * 8 + z, "narrow": lax.rem(cx, 2) * 2 + core}

    up = {"dp": lax.rem(y + 1, 4)}
    down = {"dp": lax.rem(y + 3, 4)}

    loads = [
        pltpu.make_async_copy(a, b, load_sem.at[i])
        for i, (a, b) in enumerate(
            ((tok_h, tok), (rout_h, rout), (cot_h, cot), (win_h, win), (wout_h, wout))
        )
    ]
    for c in loads:
        c.start()

    barrier = pltpu.get_barrier_semaphore()

    def greet(k, _):
        pl.semaphore_signal(
            barrier, inc=1, device_id=plane(lax.rem(me + k, 64)), device_id_type=MESH
        )
        return _

    lax.fori_loop(1, 64, greet, 0)

    def greet_far(k, _):
        q = lax.rem(y + 1 + k // 4, 4) * 4 + lax.rem(k, 4)
        pl.semaphore_signal(barrier, inc=1, device_id=chip(q), device_id_type=MESH)
        return _

    lax.fori_loop(0, 12, greet_far, 0)

    give_v[:, pl.ds(40, 8), :] = jnp.zeros((16, 8, 128), F32)
    keep_v[:, pl.ds(40, 8), :] = jnp.zeros((16, 8, 128), F32)

    def source(r):
        e = r // 16
        h = (r // 8) % 2
        c = (r // 4) % 2
        s = (r // 2) % 2
        return (h * 4 + c * 2 + r % 2) * EACH // 2 + e * 2 + s

    i0 = lax.broadcasted_iota(jnp.int32, (ROWS, ROWS), 0)
    i1 = lax.broadcasted_iota(jnp.int32, (ROWS, ROWS), 1)
    perm[...] = jnp.where(source(i0) == i1, 1.0, 0.0).astype(BF)
    perm_t[...] = jnp.where(source(i1) == i0, 1.0, 0.0).astype(BF)

    loads[0].wait()
    loads[1].wait()
    for i in range(2):
        rows = pl.ds(i * 256, 256)
        logits = dot(tok[rows, :], rout[...])
        d = jnp.exp(logits - jnp.max(logits, axis=0, keepdims=True))
        d = d / jnp.sum(d, axis=0, keepdims=True)
        c = jnp.exp(logits - jnp.max(logits, axis=1, keepdims=True))
        c = c / jnp.sum(c, axis=1, keepdims=True)
        disp[rows, :] = d
        comb[rows, :] = c
        if i == 0:
            loads[2].wait()
        for kind, (weight, values) in enumerate(((d, tok), (c, cot))):
            weight_t = weight.astype(BF).T
            for h in range(2):
                slots = dot(weight_t, values[rows, pl.ds(h * HALF, HALF)]).astype(BF)
                for g in range(PH):
                    stage[g, pl.ds((h * 4 + kind * 2 + i) * EACH // 2, EACH // 2), :] = slots[
                        g * EACH // 2 : (g + 1) * EACH // 2, :
                    ]
    for g in range(PH):
        send[pl.ds(2 * g, 2)] = dot(perm[...], stage[g]).astype(BF).reshape(2, 4, 16, HALF)

    pl.semaphore_wait(barrier, 75)

    def wait_bytes(ref, sem):
        pltpu.make_async_copy(ref, ref, sem).wait()

    def remote(src, dst, s, r, to):
        return pltpu.make_async_remote_copy(
            src_ref=src, dst_ref=dst, send_sem=s, recv_sem=r, device_id=to, device_id_type=MESH
        )

    lo, hi = pl.ds(0, 2), pl.ds(2, 2)
    ag = {}
    rs = {}

    line = pl.ds(pl.multiple_of((wide // 8) * 8, 8), 8)
    front4, rear4 = pl.ds(0, 4), pl.ds(4, 4)
    ag[0, 0] = remote(send.at[line, narrow], early.at[1], ag_send.at[0, 0], ag_recv.at[0, 0], up)
    ag[0, 1] = remote(send.at[line, narrow], early.at[3], ag_send.at[0, 1], ag_recv.at[0, 1], down)
    ag[0, 0].start()
    ag[0, 1].start()

    own = pltpu.make_async_copy(send.at[wide, narrow], recv.at[pl.ds(0, 16)], own_sem.at[0])
    own.start()

    def post_phase(p):
        def post(k, _):
            w, n = place_of(p, k, 1)
            pltpu.make_async_remote_copy(
                src_ref=send.at[w, n],
                dst_ref=recv.at[pl.ds(pl.multiple_of(k * 16, 16), 16)],
                send_sem=a2a_send.at[0],
                recv_sem=a2a_recv.at[p],
                device_id={"wide": w, "narrow": n},
                device_id_type=MESH,
            ).start()
            return _

        lax.fori_loop(MSG * p + (p == 0), MSG * p + MSG, post, 0)

    for p in (1, 2, 3, 4, 5, 6, 7, 0):
        post_phase(p)

    def forward(d):
        def post(k, _):
            w, n = place_of(0, k, 1)
            remote(
                early.at[d, lax.rem(w, 8)], spare.at[d, k], fwd_send.at[d], fwd_recv.at[d],
                {"wide": w, "narrow": n},
            ).start()
            return _

        lax.fori_loop(1, 8, post, 0)

    def early_relay():
        ag[0, 0].wait_recv()
        ag[0, 2] = remote(early.at[1, front4], early.at[2, front4], ag_send.at[0, 2], ag_recv.at[0, 2], up)
        ag[0, 2].start()
        ag[0, 1].wait_recv()
        ag[0, 3] = remote(early.at[3, rear4], early.at[2, rear4], ag_send.at[0, 3], ag_recv.at[0, 3], down)
        ag[0, 3].start()
        forward(1)
        forward(3)

    def early_last():
        ag[0, 2].wait_recv()
        ag[0, 3].wait_recv()
        forward(2)
        keep = pltpu.make_async_copy(early.at[pl.ds(1, 3), z], spare.at[pl.ds(1, 3), 0], own_sem.at[1])
        keep.start()
        keep.wait()

    def early_sort():
        own.wait()
        wait_bytes(recv.at[pl.ds(0, ROWS - 16)], a2a_recv.at[0])
        rows = dot(perm_t[...], recv[pl.ds(0, ROWS), :]).astype(BF)
        gath[0, :, 0] = rows.reshape(4, EACH, HALF)
        for d in range(1, 4):
            wait_bytes(spare.at[d, pl.ds(1, 7)], fwd_recv.at[d])
            rows = dot(perm_t[...], spare[d].reshape(ROWS, HALF)).astype(BF)
            gath[0, :, d] = rows.reshape(4, EACH, HALF)

    def stage_a(p):
        wait_bytes(recv.at[pl.ds(ROWS * p, ROWS)], a2a_recv.at[p])
        rows = dot(perm_t[...], recv[pl.ds(ROWS * p, ROWS), :]).astype(BF)
        gath[p, :, 0] = rows.reshape(4, EACH, HALF)
        ag[p, 0] = remote(gath.at[p, :, 0], gath.at[p, :, 1], ag_send.at[p, 0], ag_recv.at[p, 0], up)
        ag[p, 1] = remote(gath.at[p, :, 0], gath.at[p, :, 3], ag_send.at[p, 1], ag_recv.at[p, 1], down)
        ag[p, 0].start()
        ag[p, 1].start()

    def stage_b(p):
        ag[p, 0].wait_recv()
        ag[p, 2] = remote(gath.at[p, lo, 1], gath.at[p, lo, 2], ag_send.at[p, 2], ag_recv.at[p, 2], up)
        ag[p, 2].start()
        ag[p, 1].wait_recv()
        ag[p, 3] = remote(gath.at[p, hi, 3], gath.at[p, hi, 2], ag_send.at[p, 3], ag_recv.at[p, 3], down)
        ag[p, 3].start()

    def early_home():
        for d in range(4):
            rows = dot(perm[...], part[0, :, d].reshape(ROWS, HALF)).astype(BF)
            ret0[d] = rows.reshape(8, 16, HALF)

            def post(k, _, d=d):
                w, n = place_of(0, k, -1)
                remote(
                    ret0.at[d, k], home.at[d, z], home_send.at[0], home_recv.at[0],
                    {"wide": w, "narrow": n},
                ).start()
                return _

            lax.fori_loop(1, 8, post, 0)
        pltpu.make_async_copy(ret0.at[:, 0], home.at[:, z], own_sem.at[2]).start()

    def late_send():
        pltpu.make_async_copy(ret0.at[:, 0], home.at[:, z], own_sem.at[2]).wait()
        wait_bytes(home.at[:, pl.ds(0, 7)], home_recv.at[0])
        rs[0, 0] = remote(home.at[2, front4], home_a.at[0], rs_send.at[0, 0], rs_recv.at[0, 0], up)
        rs[0, 1] = remote(home.at[2, rear4], home_a.at[1], rs_send.at[0, 1], rs_recv.at[0, 1], down)
        rs[0, 2] = remote(home.at[3, rear4], home_b.at[rear4], rs_send.at[0, 2], rs_recv.at[0, 2], up)
        rs[0, 3] = remote(home.at[1, front4], home_c.at[front4], rs_send.at[0, 3], rs_recv.at[0, 3], down)
        for j in range(4):
            rs[0, j].start()

    def late_relay():
        rs[0, 0].wait_recv()
        home[3, front4] = (home[3, front4].astype(F32) + home_a[0].astype(F32)).astype(BF)
        rs[0, 4] = remote(home.at[3, front4], home_b.at[front4], rs_send.at[0, 4], rs_recv.at[0, 4], up)
        rs[0, 4].start()
        rs[0, 1].wait_recv()
        home[1, rear4] = (home[1, rear4].astype(F32) + home_a[1].astype(F32)).astype(BF)
        rs[0, 5] = remote(home.at[1, rear4], home_c.at[rear4], rs_send.at[0, 5], rs_recv.at[0, 5], down)
        rs[0, 5].start()

    def late_sum():
        for j in range(2, 6):
            rs[0, j].wait_recv()
        total = home[0].astype(F32) + home_b[...].astype(F32) + home_c[...].astype(F32)
        back[line, narrow] = total.astype(BF)

    def stage_c(p):
        if p > 0:
            ag[p, 2].wait_recv()
            ag[p, 3].wait_recv()
        if p == 1:
            loads[3].wait()
            loads[4].wait()
        mine = pl.ds(4 * EACH * p, 4 * EACH)

        def rows(q):
            return gath[p, q].reshape(4 * EACH, HALF)

        pre[...] = dot(rows(0), win[pl.ds(0, HALF), :]) + dot(rows(2), win[pl.ds(HALF, HALF), :])
        back_f[...] = dot_nt(rows(1), wout[:, pl.ds(0, HALF)]) + dot_nt(
            rows(3), wout[:, pl.ds(HALF, HALF)]
        )

        def nonlinear(j, _):
            r = pl.ds(pl.multiple_of(j * 16, 16), 16)
            v = pre[r, :]
            cdf, pdf = normal_cdf_pdf(v)
            to = pl.ds(pl.multiple_of(4 * EACH * p + j * 16, 16), 16)
            act[to, :] = (v * cdf).astype(BF)
            hid[to, :] = (back_f[r, :] * (cdf + v * pdf)).astype(BF)
            return _

        lax.fori_loop(0, EACH // 4, nonlinear, 0)
        for h in range(2):
            cols = pl.ds(h * HALF, HALF)
            part[p, 2 * h] = dot(act[mine, :], wout[:, cols]).astype(BF).reshape(4, EACH, HALF)
            part[p, 2 * h + 1] = dot_nt(hid[mine, :], win[cols, :]).astype(BF).reshape(4, EACH, HALF)
        if p == 0:
            early_home()
            return
        rs[p, 0] = remote(part.at[p, lo, 2], ring_a.at[p, 0], rs_send.at[p, 0], rs_recv.at[p, 0], up)
        rs[p, 1] = remote(part.at[p, hi, 2], ring_a.at[p, 1], rs_send.at[p, 1], rs_recv.at[p, 1], down)
        rs[p, 2] = remote(part.at[p, hi, 3], ring_b.at[p, hi], rs_send.at[p, 2], rs_recv.at[p, 2], up)
        rs[p, 3] = remote(part.at[p, lo, 1], ring_c.at[p, lo], rs_send.at[p, 3], rs_recv.at[p, 3], down)
        for j in range(4):
            rs[p, j].start()

    def stage_d(p):
        rs[p, 0].wait_recv()
        part[p, lo, 3] = (part[p, lo, 3].astype(F32) + ring_a[p, 0].astype(F32)).astype(BF)
        rs[p, 4] = remote(part.at[p, lo, 3], ring_b.at[p, lo], rs_send.at[p, 4], rs_recv.at[p, 4], up)
        rs[p, 4].start()
        rs[p, 1].wait_recv()
        part[p, hi, 1] = (part[p, hi, 1].astype(F32) + ring_a[p, 1].astype(F32)).astype(BF)
        rs[p, 5] = remote(part.at[p, hi, 1], ring_c.at[p, hi], rs_send.at[p, 5], rs_recv.at[p, 5], down)
        rs[p, 5].start()

    def stage_e(p):
        for j in range(2, 6):
            rs[p, j].wait_recv()
        total = part[p, :, 0].astype(F32) + ring_b[p].astype(F32) + ring_c[p].astype(F32)
        ret[pl.ds(ROWS * p, ROWS), :] = dot(perm[...], total.astype(BF).reshape(ROWS, HALF)).astype(BF)

        def post(k, _):
            w, n = place_of(p, k, -1)
            pltpu.make_async_remote_copy(
                src_ref=ret.at[pl.ds(pl.multiple_of(k * 16, 16), 16)],
                dst_ref=back.at[wide, narrow],
                send_sem=ret_send.at[0],
                recv_sem=ret_recv.at[0],
                device_id={"wide": w, "narrow": n},
                device_id_type=MESH,
            ).start()
            return _

        lax.fori_loop(MSG * p, MSG * p + MSG, post, 0)

    def grad_first(h):
        total = None
        for p in range(PH):
            term = dot_tn(
                gath[p, 2 * h].reshape(4 * EACH, HALF), hid[pl.ds(4 * EACH * p, 4 * EACH), :]
            )
            total = term if total is None else total + term
        ginv[pl.ds(h * HALF, HALF), :] = total.astype(BF)

    def grad_second(h):
        total = None
        for p in range(PH):
            term = dot_tn(
                act[pl.ds(4 * EACH * p, 4 * EACH), :], gath[p, 2 * h + 1].reshape(4 * EACH, HALF)
            )
            total = term if total is None else total + term
        goutv[:, pl.ds(h * HALF, HALF)] = total.astype(BF)

    for t in range(1, PH + 4):
        if t < PH:
            stage_a(t)
        if t == 1:
            early_relay()
        if 1 <= t - 1 < PH:
            stage_b(t - 1)
        if t == 2:
            early_last()
        if 1 <= t - 2 < PH:
            stage_c(t - 2)
        if t == 7:
            early_sort()
            stage_c(0)
        if t == PH + 1:
            late_send()
        if 1 <= t - 3 < PH:
            stage_d(t - 3)
        if 1 <= t - 4 < PH:
            stage_e(t - 4)
        if t == PH + 2:
            late_relay()
            grad_first(0)
            grad_first(1)
    grad_second(0)
    grad_second(1)
    late_sum()

    wait_bytes(back.at[pl.ds(0, 14)], ret_recv.at[0])
    for g in range(PH):
        rows = dot(perm_t[...], back[pl.ds(2 * g, 2)].reshape(ROWS, HALF)).astype(BF)
        for j in range(8):
            low[j, pl.ds(g * EACH // 2, EACH // 2), :] = rows[j * EACH // 2 : (j + 1) * EACH // 2, :]
    logit = []
    turned = []
    for i in range(2):
        rows = pl.ds(i * 256, 256)
        h0, h1 = pl.ds(0, HALF), pl.ds(HALF, HALF)
        left = dot_nt(cot[rows, h0], low[i]) + dot_nt(cot[rows, h1], low[4 + i])
        right = dot_nt(tok[rows, h0], low[2 + i]) + dot_nt(tok[rows, h1], low[6 + i])
        c, d = comb[rows, :], disp[rows, :]
        g = c * (left - jnp.sum(c * left, axis=1, keepdims=True))
        g = g + d * (right - jnp.sum(d * right, axis=0, keepdims=True))
        logit.append(g.astype(BF))
        turned.append(g.astype(BF).T)

    def router_half(which):
        cols = pl.ds(pl.multiple_of(which * HALF, HALF), HALF)
        term = dot(turned[0], tok[pl.ds(0, 256), cols]) + dot(turned[1], tok[pl.ds(256, 256), cols])
        return term.T.reshape(16, 40, 128)

    sibling = {"narrow": narrow + 1 - 2 * core}
    give_v[:, pl.ds(0, 40), :] = router_half(1 - core)
    first = remote(give_v, ar0, ar_send.at[0], ar_recv.at[0], sibling)
    first.start()
    keep_v[:, pl.ds(0, 40), :] = router_half(core)

    def image_out(i):
        rows = pl.ds(i * 256, 256)
        dl = disp[rows, :].astype(BF)
        cl = comb[rows, :].astype(BF)
        for h in range(2):
            cols = pl.ds(h * HALF, HALF)
            mixed[rows, cols] = dot(cl, low[h * 4 + i]).astype(BF)
            tgrad[rows, cols] = (
                dot(dl, low[h * 4 + 2 + i]) + dot_nt(logit[i], rout[cols, :])
            ).astype(BF)

    first.wait_recv()
    half[...] = (keep_v[...] + ar0[...]).astype(BF)

    def scatter(j, _):
        q = lax.rem(spot + j, 16)
        remote(half.at[q], ar1.at[j], ar_send.at[1], ar_recv.at[1], chip(q)).start()
        return _

    lax.fori_loop(1, 16, scatter, 0)
    image_out(0)
    wait_bytes(ar1.at[pl.ds(1, 15)], ar_recv.at[1])
    total = half[spot].astype(F32)
    for j in range(1, 16):
        total = total + ar1[j].astype(F32)
    one[...] = total.astype(BF)
    ar2[z] = total.astype(BF)

    def across(j, _):
        to = (wide // 8) * 8 + lax.rem(z + j, 8)
        remote(one, ar2.at[z], ar_send.at[2], ar_recv.at[2], {"wide": to}).start()
        return _

    lax.fori_loop(1, 8, across, 0)
    image_out(1)
    wait_bytes(ar2.at[pl.ds(0, 7)], ar_recv.at[2])
    total = ar2[0].astype(F32)
    for j in range(1, 8):
        total = total + ar2[j].astype(F32)
    whole[core, spot] = total.astype(BF)

    def spread(j, _):
        mine = whole.at[core, spot]
        remote(mine, mine, ar_send.at[3], ar_recv.at[3], chip(lax.rem(spot + j, 16))).start()
        return _

    lax.fori_loop(1, 16, spread, 0)
    wait_bytes(ar1.at[pl.ds(1, 15)], ar_recv.at[3])
    last = remote(whole.at[core], whole.at[core], ar_send.at[4], ar_recv.at[4], sibling)
    last.start()
    fin[core] = whole[core].astype(F32)[:, :40, :]
    last.wait_recv()
    fin[1 - core] = whole[1 - core].astype(F32)[:, :40, :]

    wait_bytes(recv.at[pl.ds(0, 63 * 16)], a2a_send.at[0])
    wait_bytes(recv.at[pl.ds(0, 56 * 16)], ret_send.at[0])
    for d in range(1, 4):
        wait_bytes(spare.at[d, pl.ds(1, 7)], fwd_send.at[d])
    wait_bytes(home.at[:, pl.ds(0, 7)], home_send.at[0])
    for c in list(ag.values()) + list(rs.values()):
        c.wait_send()
    first.wait_send()
    last.wait_send()
    wait_bytes(ar1.at[pl.ds(1, 15)], ar_send.at[1])
    wait_bytes(ar2.at[pl.ds(0, 7)], ar_send.at[2])
    wait_bytes(ar1.at[pl.ds(1, 15)], ar_send.at[3])


def write_out(*refs):
    sem = refs[-1]
    copies = [pltpu.make_async_copy(refs[i], refs[5 + i], sem.at[i]) for i in range(5)]
    for c in copies:
        c.start()
    for c in copies:
        c.wait()


def local(tokens, router, expert_in, expert_out, cotangent):
    images, length, width = tokens.shape
    slots = router.shape[1]
    hidden = expert_in.shape[2]
    rows = images * length
    vm = pltpu.VMEM
    dma = pltpu.SemaphoreType.DMA
    anywhere = pl.BlockSpec(memory_space=pl.ANY)
    outs = (
        jax.ShapeDtypeStruct((rows, width), BF),
        jax.ShapeDtypeStruct((rows, width), BF),
        jax.ShapeDtypeStruct((2, 16, 40, slots), F32),
        jax.ShapeDtypeStruct((width, hidden), BF),
        jax.ShapeDtypeStruct((hidden, width), BF),
    )
    out = pl.pallas_call(
        kernel,
        out_shape=tuple(pltpu.VMEM(o.shape, o.dtype) for o in outs),
        in_specs=[anywhere] * 5,
        out_specs=[pl.BlockSpec(memory_space=pltpu.VMEM)] * 5,
        scratch_shapes=[
            vm((rows, width), BF), vm((width, slots), BF), vm((width, hidden), BF),
            vm((hidden, width), BF), vm((rows, width), BF),
            vm((ROWS, ROWS), BF), vm((ROWS, ROWS), BF),
            vm((rows, slots), F32), vm((rows, slots), F32),
            vm((PH, ROWS, HALF), BF), vm((16, 4, 16, HALF), BF), vm((1024, HALF), BF),
            vm((PH, 4, 4, EACH, HALF), BF), vm((PH, 4, 4, EACH, HALF), BF),
            vm((PH, 2, 2, EACH, HALF), BF),
            vm((PH, 4, EACH, HALF), BF), vm((PH, 4, EACH, HALF), BF),
            vm((4 * EACH, hidden), F32), vm((4 * EACH, hidden), F32),
            vm((1024, hidden), BF), vm((1024, hidden), BF),
            vm((1024, HALF), BF), vm((16, 4, 16, HALF), BF),
            vm((8, 128, HALF), BF),
            vm((4, 8, 16, HALF), BF), vm((4, 8, 16, HALF), BF),
            vm((4, 8, 16, HALF), BF), vm((4, 8, 16, HALF), BF),
            vm((2, 4, 16, HALF), BF), vm((8, 16, HALF), BF), vm((8, 16, HALF), BF),
            vm((16, 48, slots), F32), vm((16, 48, slots), F32), vm((16, 48, slots), F32),
            vm((16, 48, slots), BF), vm((16, 48, slots), BF),
            vm((48, slots), BF), vm((8, 48, slots), BF), vm((2, 16, 48, slots), BF),
            dma((5,)), dma((3,)), dma((1,)), dma((PH,)),
            dma((PH, 4)), dma((PH, 4)), dma((PH, 6)), dma((PH, 6)),
            dma((1,)), dma((1,)), dma((4,)), dma((4,)), dma((1,)), dma((1,)), dma((5,)), dma((5,)),
        ],
        compiler_params=pltpu.CompilerParams(
            collective_id=0, has_side_effects=True, vmem_limit_bytes=50 * 1024 * 1024
        ),
        cost_estimate=pl.CostEstimate(
            flops=12 * 10**9, bytes_accessed=12 * 10**6, transcendentals=2 * 10**6
        ),
    )(
        tokens.reshape(rows, width), router, expert_in[0], expert_out[0],
        cotangent.reshape(rows, width),
    )
    out = pl.pallas_call(
        write_out,
        out_shape=outs,
        in_specs=[pl.BlockSpec(memory_space=pltpu.VMEM)] * 5,
        out_specs=[anywhere] * 5,
        scratch_shapes=[dma((5,))],
        compiler_params=pltpu.CompilerParams(vmem_limit_bytes=1024 * 1024),
    )(*out)
    mixed, token_grad, router_grad, grad_in, grad_out = out
    return (
        mixed.reshape(images, length, width),
        token_grad.reshape(images, length, width),
        router_grad.reshape(width, slots),
        grad_in[None],
        grad_out[None],
    )


def solution(mesh):
    in_specs = (
        P(("dp", "wide", "narrow"), None, None),
        P(),
        P(("wide", "narrow"), None, "dp"),
        P(("wide", "narrow"), "dp", None),
        P(("dp", "wide", "narrow"), None, None),
    )
    out_specs = (
        P(("dp", "wide", "narrow"), None, None),
        P(("dp", "wide", "narrow"), None, None),
        P(),
        P(("wide", "narrow"), None, "dp"),
        P(("wide", "narrow"), "dp", None),
    )
    return jax.shard_map(local, mesh=mesh, in_specs=in_specs, out_specs=out_specs, check_vma=False)
```

```python
import functools

import jax
import jax.numpy as jnp
from jax import lax
from jax.experimental import pallas as pl
from jax.experimental.pallas import tpu as pltpu
from jax.sharding import PartitionSpec as P

MESH = pl.DeviceIdType.MESH
BF = jnp.bfloat16
F32 = jnp.float32
FAR16 = sorted(range(1, 16), key=lambda j: -min(j % 4, 4 - j % 4) - min(j // 4, 4 - j // 4))
FAR8 = (4, 3, 5, 2, 6, 1, 7)
PH = 8
MSG = 64 // PH
ROWS = 16 * MSG
EACH = ROWS // 4
STEPS = ((0, 0), (0, 1), (1, 0), (1, 1), (2, 0), (2, 1), (3, 0), (3, 1))
HALF = 640


def dot(a, b):
    return jnp.dot(a, b, preferred_element_type=F32)


def dot_nt(a, b):
    return lax.dot_general(a, b, (((1,), (1,)), ((), ())), preferred_element_type=F32)


def dot_tn(a, b):
    return lax.dot_general(a, b, (((0,), (0,)), ((), ())), preferred_element_type=F32)


def normal_cdf_pdf(x):
    z = jnp.abs(x) * 0.7071067811865476
    t = 1.0 / (1.0 + 0.5 * z)
    poly = 0.17087277
    for c in (
        -0.82215223,
        1.48851587,
        -1.13520398,
        0.27886807,
        -0.18628806,
        0.09678418,
        0.37409196,
        1.00002368,
        -1.26551223,
    ):
        poly = poly * t + c
    square = z * z
    tail = 0.5 * t * jnp.exp(poly - square)
    cdf = jnp.where(x < 0, tail, 1.0 - tail)
    pdf = 0.3989422804014327 * jnp.exp(-square)
    return cdf, pdf


def kernel(
    tok_h, rout_h, win_h, wout_h, cot_h,
    mixed, tgrad, fin, ginv, goutv,
    tok, rout, win, wout, cot,
    perm, perm_t, disp, comb, stage, send, recv, gath, part, ring_a, ring_b, ring_c,
    pre, back_f, act, hid, ret, back, low,
    early, spare, ret0, home, home_a, home_b, home_c,
    give_v, keep_v, ar0, half, ar1, one, ar2, whole,
    load_sem, own_sem, a2a_send, a2a_recv, ag_send, ag_recv, rs_send, rs_recv,
    ret_send, ret_recv, fwd_send, fwd_recv, home_send, home_recv, ar_send, ar_recv,
):
    y = lax.axis_index("dp")
    wide = lax.axis_index("wide")
    narrow = lax.axis_index("narrow")
    me = wide * 4 + narrow
    z = lax.rem(wide, 8)
    x = (wide // 8) * 2 + narrow // 2
    core = lax.rem(narrow, 2)
    spot = y * 4 + x

    def plane(e):
        return {"wide": e // 4, "narrow": lax.rem(e, 4)}

    def place_of(p, k, sign):
        dx, dc = STEPS[p]
        j = lax.rem(k, 8)
        dz = (j % 2) * ((j + 1) // 2) + (1 - j % 2) * (8 - j // 2)
        px = (x + sign * dx + 4) % 4
        pz = (z + sign * dz + 8) % 8
        pc = (core + dc) % 2
        return (px // 2) * 8 + pz, (px % 2) * 2 + pc

    def chip(q):
        cx = lax.rem(q, 4)
        return {"dp": q // 4, "wide": (cx // 2) * 8 + z, "narrow": lax.rem(cx, 2) * 2 + core}

    up = {"dp": lax.rem(y + 1, 4)}
    down = {"dp": lax.rem(y + 3, 4)}

    loads = [
        pltpu.make_async_copy(a, b, load_sem.at[i])
        for i, (a, b) in enumerate(
            ((tok_h, tok), (rout_h, rout), (cot_h, cot), (win_h, win), (wout_h, wout))
        )
    ]
    for c in loads:
        c.start()

    barrier = pltpu.get_barrier_semaphore()

    def greet(k, _):
        pl.semaphore_signal(
            barrier, inc=1, device_id=plane(lax.rem(me + k, 64)), device_id_type=MESH
        )
        return _

    lax.fori_loop(1, 64, greet, 0)

    def greet_far(k, _):
        q = lax.rem(y + 1 + k // 4, 4) * 4 + lax.rem(k, 4)
        pl.semaphore_signal(barrier, inc=1, device_id=chip(q), device_id_type=MESH)
        return _

    lax.fori_loop(0, 12, greet_far, 0)

    give_v[:, pl.ds(40, 8), :] = jnp.zeros((16, 8, 128), F32)
    keep_v[:, pl.ds(40, 8), :] = jnp.zeros((16, 8, 128), F32)

    def source(r):
        e = r // 16
        h = (r // 8) % 2
        c = (r // 4) % 2
        s = (r // 2) % 2
        return (h * 4 + c * 2 + r % 2) * EACH // 2 + e * 2 + s

    i0 = lax.broadcasted_iota(jnp.int32, (ROWS, ROWS), 0)
    i1 = lax.broadcasted_iota(jnp.int32, (ROWS, ROWS), 1)
    perm[...] = jnp.where(source(i0) == i1, 1.0, 0.0).astype(BF)
    perm_t[...] = jnp.where(source(i1) == i0, 1.0, 0.0).astype(BF)

    loads[0].wait()
    loads[1].wait()
    for i in range(2):
        rows = pl.ds(i * 256, 256)
        logits = dot(tok[rows, :], rout[...])
        d = jnp.exp(logits - jnp.max(logits, axis=0, keepdims=True))
        d = d / jnp.sum(d, axis=0, keepdims=True)
        c = jnp.exp(logits - jnp.max(logits, axis=1, keepdims=True))
        c = c / jnp.sum(c, axis=1, keepdims=True)
        disp[rows, :] = d
        comb[rows, :] = c
        if i == 0:
            loads[2].wait()
        for kind, (weight, values) in enumerate(((d, tok), (c, cot))):
            weight_t = weight.astype(BF).T
            for h in range(2):
                slots = dot(weight_t, values[rows, pl.ds(h * HALF, HALF)]).astype(BF)
                for g in range(PH):
                    stage[g, pl.ds((h * 4 + kind * 2 + i) * EACH // 2, EACH // 2), :] = slots[
                        g * EACH // 2 : (g + 1) * EACH // 2, :
                    ]
    for g in range(PH):
        send[pl.ds(2 * g, 2)] = dot(perm[...], stage[g]).astype(BF).reshape(2, 4, 16, HALF)

    pl.semaphore_wait(barrier, 75)

    def wait_bytes(ref, sem):
        pltpu.make_async_copy(ref, ref, sem).wait()

    def remote(src, dst, s, r, to):
        return pltpu.make_async_remote_copy(
            src_ref=src, dst_ref=dst, send_sem=s, recv_sem=r, device_id=to, device_id_type=MESH
        )

    lo, hi = pl.ds(0, 2), pl.ds(2, 2)
    ag = {}
    rs = {}

    line = pl.ds(pl.multiple_of((wide // 8) * 8, 8), 8)
    front4, rear4 = pl.ds(0, 4), pl.ds(4, 4)
    ag[0, 0] = remote(send.at[line, narrow], early.at[1], ag_send.at[0, 0], ag_recv.at[0, 0], up)
    ag[0, 1] = remote(send.at[line, narrow], early.at[3], ag_send.at[0, 1], ag_recv.at[0, 1], down)
    ag[0, 0].start()
    ag[0, 1].start()

    own = pltpu.make_async_copy(send.at[wide, narrow], recv.at[pl.ds(0, 16)], own_sem.at[0])
    own.start()

    def post_phase(p):
        def post(k, _):
            w, n = place_of(p, k, 1)
            pltpu.make_async_remote_copy(
                src_ref=send.at[w, n],
                dst_ref=recv.at[pl.ds(pl.multiple_of(k * 16, 16), 16)],
                send_sem=a2a_send.at[0],
                recv_sem=a2a_recv.at[p],
                device_id={"wide": w, "narrow": n},
                device_id_type=MESH,
            ).start()
            return _

        lax.fori_loop(MSG * p + (p == 0), MSG * p + MSG, post, 0)

    for p in (1, 2, 3, 4, 5, 6, 7, 0):
        post_phase(p)

    def forward(d):
        def post(k, _):
            w, n = place_of(0, k, 1)
            remote(
                early.at[d, lax.rem(w, 8)], spare.at[d, k], fwd_send.at[d], fwd_recv.at[d],
                {"wide": w, "narrow": n},
            ).start()
            return _

        lax.fori_loop(1, 8, post, 0)

    def early_relay():
        ag[0, 0].wait_recv()
        ag[0, 2] = remote(early.at[1, front4], early.at[2, front4], ag_send.at[0, 2], ag_recv.at[0, 2], up)
        ag[0, 2].start()
        ag[0, 1].wait_recv()
        ag[0, 3] = remote(early.at[3, rear4], early.at[2, rear4], ag_send.at[0, 3], ag_recv.at[0, 3], down)
        ag[0, 3].start()
        forward(1)
        forward(3)

    def early_last():
        ag[0, 2].wait_recv()
        ag[0, 3].wait_recv()
        forward(2)
        keep = pltpu.make_async_copy(early.at[pl.ds(1, 3), z], spare.at[pl.ds(1, 3), 0], own_sem.at[1])
        keep.start()
        keep.wait()

    def early_sort():
        own.wait()
        wait_bytes(recv.at[pl.ds(0, ROWS - 16)], a2a_recv.at[0])
        rows = dot(perm_t[...], recv[pl.ds(0, ROWS), :]).astype(BF)
        gath[0, :, 0] = rows.reshape(4, EACH, HALF)
        for d in range(1, 4):
            wait_bytes(spare.at[d, pl.ds(1, 7)], fwd_recv.at[d])
            rows = dot(perm_t[...], spare[d].reshape(ROWS, HALF)).astype(BF)
            gath[0, :, d] = rows.reshape(4, EACH, HALF)

    def stage_a(p):
        wait_bytes(recv.at[pl.ds(ROWS * p, ROWS)], a2a_recv.at[p])
        rows = dot(perm_t[...], recv[pl.ds(ROWS * p, ROWS), :]).astype(BF)
        gath[p, :, 0] = rows.reshape(4, EACH, HALF)
        ag[p, 0] = remote(gath.at[p, :, 0], gath.at[p, :, 1], ag_send.at[p, 0], ag_recv.at[p, 0], up)
        ag[p, 1] = remote(gath.at[p, :, 0], gath.at[p, :, 3], ag_send.at[p, 1], ag_recv.at[p, 1], down)
        ag[p, 0].start()
        ag[p, 1].start()

    def stage_b(p):
        ag[p, 0].wait_recv()
        ag[p, 2] = remote(gath.at[p, lo, 1], gath.at[p, lo, 2], ag_send.at[p, 2], ag_recv.at[p, 2], up)
        ag[p, 2].start()
        ag[p, 1].wait_recv()
        ag[p, 3] = remote(gath.at[p, hi, 3], gath.at[p, hi, 2], ag_send.at[p, 3], ag_recv.at[p, 3], down)
        ag[p, 3].start()

    def early_home():
        for d in range(4):
            rows = dot(perm[...], part[0, :, d].reshape(ROWS, HALF)).astype(BF)
            ret0[d] = rows.reshape(8, 16, HALF)

            def post(k, _, d=d):
                w, n = place_of(0, k, -1)
                remote(
                    ret0.at[d, k], home.at[d, z], home_send.at[0], home_recv.at[0],
                    {"wide": w, "narrow": n},
                ).start()
                return _

            lax.fori_loop(1, 8, post, 0)
        pltpu.make_async_copy(ret0.at[:, 0], home.at[:, z], own_sem.at[2]).start()

    def late_send():
        pltpu.make_async_copy(ret0.at[:, 0], home.at[:, z], own_sem.at[2]).wait()
        wait_bytes(home.at[:, pl.ds(0, 7)], home_recv.at[0])
        rs[0, 0] = remote(home.at[2, front4], home_a.at[0], rs_send.at[0, 0], rs_recv.at[0, 0], up)
        rs[0, 1] = remote(home.at[2, rear4], home_a.at[1], rs_send.at[0, 1], rs_recv.at[0, 1], down)
        rs[0, 2] = remote(home.at[3, rear4], home_b.at[rear4], rs_send.at[0, 2], rs_recv.at[0, 2], up)
        rs[0, 3] = remote(home.at[1, front4], home_c.at[front4], rs_send.at[0, 3], rs_recv.at[0, 3], down)
        for j in range(4):
            rs[0, j].start()

    def late_relay():
        rs[0, 0].wait_recv()
        home[3, front4] = (home[3, front4].astype(F32) + home_a[0].astype(F32)).astype(BF)
        rs[0, 4] = remote(home.at[3, front4], home_b.at[front4], rs_send.at[0, 4], rs_recv.at[0, 4], up)
        rs[0, 4].start()
        rs[0, 1].wait_recv()
        home[1, rear4] = (home[1, rear4].astype(F32) + home_a[1].astype(F32)).astype(BF)
        rs[0, 5] = remote(home.at[1, rear4], home_c.at[rear4], rs_send.at[0, 5], rs_recv.at[0, 5], down)
        rs[0, 5].start()

    def late_sum():
        for j in range(2, 6):
            rs[0, j].wait_recv()
        total = home[0].astype(F32) + home_b[...].astype(F32) + home_c[...].astype(F32)
        back[line, narrow] = total.astype(BF)

    def stage_c(p):
        if p > 0:
            ag[p, 2].wait_recv()
            ag[p, 3].wait_recv()
        if p == 1:
            loads[3].wait()
            loads[4].wait()
        mine = pl.ds(4 * EACH * p, 4 * EACH)

        def rows(q):
            return gath[p, q].reshape(4 * EACH, HALF)

        pre[...] = dot(rows(0), win[pl.ds(0, HALF), :]) + dot(rows(2), win[pl.ds(HALF, HALF), :])
        back_f[...] = dot_nt(rows(1), wout[:, pl.ds(0, HALF)]) + dot_nt(
            rows(3), wout[:, pl.ds(HALF, HALF)]
        )

        def nonlinear(j, _):
            r = pl.ds(pl.multiple_of(j * 16, 16), 16)
            v = pre[r, :]
            cdf, pdf = normal_cdf_pdf(v)
            to = pl.ds(pl.multiple_of(4 * EACH * p + j * 16, 16), 16)
            act[to, :] = (v * cdf).astype(BF)
            hid[to, :] = (back_f[r, :] * (cdf + v * pdf)).astype(BF)
            return _

        lax.fori_loop(0, EACH // 4, nonlinear, 0)
        for h in range(2):
            cols = pl.ds(h * HALF, HALF)
            part[p, 2 * h] = dot(act[mine, :], wout[:, cols]).astype(BF).reshape(4, EACH, HALF)
            part[p, 2 * h + 1] = dot_nt(hid[mine, :], win[cols, :]).astype(BF).reshape(4, EACH, HALF)
        if p == 0:
            early_home()
            return
        rs[p, 0] = remote(part.at[p, lo, 2], ring_a.at[p, 0], rs_send.at[p, 0], rs_recv.at[p, 0], up)
        rs[p, 1] = remote(part.at[p, hi, 2], ring_a.at[p, 1], rs_send.at[p, 1], rs_recv.at[p, 1], down)
        rs[p, 2] = remote(part.at[p, hi, 3], ring_b.at[p, hi], rs_send.at[p, 2], rs_recv.at[p, 2], up)
        rs[p, 3] = remote(part.at[p, lo, 1], ring_c.at[p, lo], rs_send.at[p, 3], rs_recv.at[p, 3], down)
        for j in range(4):
            rs[p, j].start()

    def stage_d(p):
        rs[p, 0].wait_recv()
        part[p, lo, 3] = (part[p, lo, 3].astype(F32) + ring_a[p, 0].astype(F32)).astype(BF)
        rs[p, 4] = remote(part.at[p, lo, 3], ring_b.at[p, lo], rs_send.at[p, 4], rs_recv.at[p, 4], up)
        rs[p, 4].start()
        rs[p, 1].wait_recv()
        part[p, hi, 1] = (part[p, hi, 1].astype(F32) + ring_a[p, 1].astype(F32)).astype(BF)
        rs[p, 5] = remote(part.at[p, hi, 1], ring_c.at[p, hi], rs_send.at[p, 5], rs_recv.at[p, 5], down)
        rs[p, 5].start()

    def stage_e(p):
        for j in range(2, 6):
            rs[p, j].wait_recv()
        total = part[p, :, 0].astype(F32) + ring_b[p].astype(F32) + ring_c[p].astype(F32)
        ret[pl.ds(ROWS * p, ROWS), :] = dot(perm[...], total.astype(BF).reshape(ROWS, HALF)).astype(BF)

        def post(k, _):
            w, n = place_of(p, k, -1)
            pltpu.make_async_remote_copy(
                src_ref=ret.at[pl.ds(pl.multiple_of(k * 16, 16), 16)],
                dst_ref=back.at[wide, narrow],
                send_sem=ret_send.at[0],
                recv_sem=ret_recv.at[0],
                device_id={"wide": w, "narrow": n},
                device_id_type=MESH,
            ).start()
            return _

        lax.fori_loop(MSG * p, MSG * p + MSG, post, 0)

    def grad_first(h):
        total = None
        for p in range(PH):
            term = dot_tn(
                gath[p, 2 * h].reshape(4 * EACH, HALF), hid[pl.ds(4 * EACH * p, 4 * EACH), :]
            )
            total = term if total is None else total + term
        ginv[pl.ds(h * HALF, HALF), :] = total.astype(BF)

    def grad_second(h):
        total = None
        for p in range(PH):
            term = dot_tn(
                act[pl.ds(4 * EACH * p, 4 * EACH), :], gath[p, 2 * h + 1].reshape(4 * EACH, HALF)
            )
            total = term if total is None else total + term
        goutv[:, pl.ds(h * HALF, HALF)] = total.astype(BF)

    for t in range(1, PH + 4):
        if t < PH:
            stage_a(t)
        if t == 1:
            early_relay()
        if 1 <= t - 1 < PH:
            stage_b(t - 1)
        if t == 2:
            early_last()
        if 1 <= t - 2 < PH:
            stage_c(t - 2)
        if t == 7:
            early_sort()
            stage_c(0)
        if 1 <= t - 3 < PH:
            stage_d(t - 3)
        if 1 <= t - 4 < PH:
            stage_e(t - 4)
        if t == PH + 1:
            late_send()
        if t == PH + 2:
            late_relay()
            grad_first(0)
            grad_first(1)
    grad_second(0)
    grad_second(1)
    late_sum()

    wait_bytes(back.at[pl.ds(0, 14)], ret_recv.at[0])
    for g in range(PH):
        rows = dot(perm_t[...], back[pl.ds(2 * g, 2)].reshape(ROWS, HALF)).astype(BF)
        for j in range(8):
            low[j, pl.ds(g * EACH // 2, EACH // 2), :] = rows[j * EACH // 2 : (j + 1) * EACH // 2, :]
    logit = []
    turned = []
    for i in range(2):
        rows = pl.ds(i * 256, 256)
        h0, h1 = pl.ds(0, HALF), pl.ds(HALF, HALF)
        left = dot_nt(cot[rows, h0], low[i]) + dot_nt(cot[rows, h1], low[4 + i])
        right = dot_nt(tok[rows, h0], low[2 + i]) + dot_nt(tok[rows, h1], low[6 + i])
        c, d = comb[rows, :], disp[rows, :]
        g = c * (left - jnp.sum(c * left, axis=1, keepdims=True))
        g = g + d * (right - jnp.sum(d * right, axis=0, keepdims=True))
        logit.append(g.astype(BF))
        turned.append(g.astype(BF).T)

    def router_half(which):
        cols = pl.ds(pl.multiple_of(which * HALF, HALF), HALF)
        term = dot(turned[0], tok[pl.ds(0, 256), cols]) + dot(turned[1], tok[pl.ds(256, 256), cols])
        return term.T.reshape(16, 40, 128)

    sibling = {"narrow": narrow + 1 - 2 * core}
    give_v[:, pl.ds(0, 40), :] = router_half(1 - core)
    first = remote(give_v, ar0, ar_send.at[0], ar_recv.at[0], sibling)
    first.start()
    keep_v[:, pl.ds(0, 40), :] = router_half(core)

    def image_out(i):
        rows = pl.ds(i * 256, 256)
        dl = disp[rows, :].astype(BF)
        cl = comb[rows, :].astype(BF)
        for h in range(2):
            cols = pl.ds(h * HALF, HALF)
            mixed[rows, cols] = dot(cl, low[h * 4 + i]).astype(BF)
            tgrad[rows, cols] = (
                dot(dl, low[h * 4 + 2 + i]) + dot_nt(logit[i], rout[cols, :])
            ).astype(BF)

    first.wait_recv()
    half[...] = (keep_v[...] + ar0[...]).astype(BF)

    def chip_at(j):
        return lax.rem(y + j // 4, 4) * 4 + lax.rem(x + j % 4, 4)

    for j in FAR16:
        q = chip_at(j)
        remote(half.at[q], ar1.at[j], ar_send.at[1], ar_recv.at[1], chip(q)).start()
    image_out(0)
    wait_bytes(ar1.at[pl.ds(1, 15)], ar_recv.at[1])
    total = half[spot].astype(F32)
    for j in range(1, 16):
        total = total + ar1[j].astype(F32)
    one[...] = total.astype(BF)
    ar2[z] = total.astype(BF)

    for j in FAR8:
        to = (wide // 8) * 8 + lax.rem(z + j, 8)
        remote(one, ar2.at[z], ar_send.at[2], ar_recv.at[2], {"wide": to}).start()
    image_out(1)
    wait_bytes(ar2.at[pl.ds(0, 7)], ar_recv.at[2])
    total = ar2[0].astype(F32)
    for j in range(1, 8):
        total = total + ar2[j].astype(F32)
    whole[core, spot] = total.astype(BF)

    mine = whole.at[core, spot]
    for j in FAR16:
        remote(mine, mine, ar_send.at[3], ar_recv.at[3], chip(chip_at(j))).start()
    wait_bytes(ar1.at[pl.ds(1, 15)], ar_recv.at[3])
    last = remote(whole.at[core], whole.at[core], ar_send.at[4], ar_recv.at[4], sibling)
    last.start()
    fin[core] = whole[core].astype(F32)[:, :40, :]
    last.wait_recv()
    fin[1 - core] = whole[1 - core].astype(F32)[:, :40, :]

    wait_bytes(recv.at[pl.ds(0, 63 * 16)], a2a_send.at[0])
    wait_bytes(recv.at[pl.ds(0, 56 * 16)], ret_send.at[0])
    for d in range(1, 4):
        wait_bytes(spare.at[d, pl.ds(1, 7)], fwd_send.at[d])
    wait_bytes(home.at[:, pl.ds(0, 7)], home_send.at[0])
    for c in list(ag.values()) + list(rs.values()):
        c.wait_send()
    first.wait_send()
    last.wait_send()
    wait_bytes(ar1.at[pl.ds(1, 15)], ar_send.at[1])
    wait_bytes(ar2.at[pl.ds(0, 7)], ar_send.at[2])
    wait_bytes(ar1.at[pl.ds(1, 15)], ar_send.at[3])


def write_out(*refs):
    sem = refs[-1]
    copies = [pltpu.make_async_copy(refs[i], refs[5 + i], sem.at[i]) for i in range(5)]
    for c in copies:
        c.start()
    for c in copies:
        c.wait()


def local(tokens, router, expert_in, expert_out, cotangent):
    images, length, width = tokens.shape
    slots = router.shape[1]
    hidden = expert_in.shape[2]
    rows = images * length
    vm = pltpu.VMEM
    dma = pltpu.SemaphoreType.DMA
    anywhere = pl.BlockSpec(memory_space=pl.ANY)
    outs = (
        jax.ShapeDtypeStruct((rows, width), BF),
        jax.ShapeDtypeStruct((rows, width), BF),
        jax.ShapeDtypeStruct((2, 16, 40, slots), F32),
        jax.ShapeDtypeStruct((width, hidden), BF),
        jax.ShapeDtypeStruct((hidden, width), BF),
    )
    out = pl.pallas_call(
        kernel,
        out_shape=tuple(pltpu.VMEM(o.shape, o.dtype) for o in outs),
        in_specs=[anywhere] * 5,
        out_specs=[pl.BlockSpec(memory_space=pltpu.VMEM)] * 5,
        scratch_shapes=[
            vm((rows, width), BF), vm((width, slots), BF), vm((width, hidden), BF),
            vm((hidden, width), BF), vm((rows, width), BF),
            vm((ROWS, ROWS), BF), vm((ROWS, ROWS), BF),
            vm((rows, slots), F32), vm((rows, slots), F32),
            vm((PH, ROWS, HALF), BF), vm((16, 4, 16, HALF), BF), vm((1024, HALF), BF),
            vm((PH, 4, 4, EACH, HALF), BF), vm((PH, 4, 4, EACH, HALF), BF),
            vm((PH, 2, 2, EACH, HALF), BF),
            vm((PH, 4, EACH, HALF), BF), vm((PH, 4, EACH, HALF), BF),
            vm((4 * EACH, hidden), F32), vm((4 * EACH, hidden), F32),
            vm((1024, hidden), BF), vm((1024, hidden), BF),
            vm((1024, HALF), BF), vm((16, 4, 16, HALF), BF),
            vm((8, 128, HALF), BF),
            vm((4, 8, 16, HALF), BF), vm((4, 8, 16, HALF), BF),
            vm((4, 8, 16, HALF), BF), vm((4, 8, 16, HALF), BF),
            vm((2, 4, 16, HALF), BF), vm((8, 16, HALF), BF), vm((8, 16, HALF), BF),
            vm((16, 48, slots), F32), vm((16, 48, slots), F32), vm((16, 48, slots), F32),
            vm((16, 48, slots), BF), vm((16, 48, slots), BF),
            vm((48, slots), BF), vm((8, 48, slots), BF), vm((2, 16, 48, slots), BF),
            dma((5,)), dma((3,)), dma((1,)), dma((PH,)),
            dma((PH, 4)), dma((PH, 4)), dma((PH, 6)), dma((PH, 6)),
            dma((1,)), dma((1,)), dma((4,)), dma((4,)), dma((1,)), dma((1,)), dma((5,)), dma((5,)),
        ],
        compiler_params=pltpu.CompilerParams(
            collective_id=0, has_side_effects=True, vmem_limit_bytes=50 * 1024 * 1024
        ),
        cost_estimate=pl.CostEstimate(
            flops=12 * 10**9, bytes_accessed=12 * 10**6, transcendentals=2 * 10**6
        ),
    )(
        tokens.reshape(rows, width), router, expert_in[0], expert_out[0],
        cotangent.reshape(rows, width),
    )
    out = pl.pallas_call(
        write_out,
        out_shape=outs,
        in_specs=[pl.BlockSpec(memory_space=pltpu.VMEM)] * 5,
        out_specs=[anywhere] * 5,
        scratch_shapes=[dma((5,))],
        compiler_params=pltpu.CompilerParams(vmem_limit_bytes=1024 * 1024),
    )(*out)
    mixed, token_grad, router_grad, grad_in, grad_out = out
    return (
        mixed.reshape(images, length, width),
        token_grad.reshape(images, length, width),
        router_grad.reshape(width, slots),
        grad_in[None],
        grad_out[None],
    )


def solution(mesh):
    in_specs = (
        P(("dp", "wide", "narrow"), None, None),
        P(),
        P(("wide", "narrow"), None, "dp"),
        P(("wide", "narrow"), "dp", None),
        P(("dp", "wide", "narrow"), None, None),
    )
    out_specs = (
        P(("dp", "wide", "narrow"), None, None),
        P(("dp", "wide", "narrow"), None, None),
        P(),
        P(("wide", "narrow"), None, "dp"),
        P(("wide", "narrow"), "dp", None),
    )
    return jax.shard_map(local, mesh=mesh, in_specs=in_specs, out_specs=out_specs, check_vma=False)
```
